256 devices in a mesh: section: 2 (over y_lo), ctx: 32 (over z, x), tp: 4 (over y_hi, core).
Axes of the slice: x: 4, y: 4 (y_hi: 2, y_lo: 2; y = y_hi * 2 + y_lo), z: 8, core: 2. Of those that a mesh axis runs over, the one named last changes fastest.
Arguments:
- frames: bfloat16 [2, 2048, 1280], P('section', 'ctx'), may hold values from -6 to 6
- proj_w: bfloat16 [1280, 1024], P(('section', 'ctx'), 'tp'), may hold values from -0.15625 to 0.15625
- text_q: bfloat16 [2, 4096, 4096], P('section', 'ctx', 'tp'), may hold values from -6 to 6, as said below
- text_k: bfloat16 [2, 4096, 512], P('section', 'ctx', 'tp'), may hold values from -6 to 6, as said below
- text_v: bfloat16 [2, 4096, 512], P('section', 'ctx', 'tp'), may hold values from -6 to 6
- frame_count: int32 [2, 32], P('section', 'ctx'), may hold values from 16 to 64, as said below
- text_len: int32 [2, 32], P('section', 'ctx'), may hold values from 32 to 128, as said below
- grad_out: bfloat16 [2, 4096, 4096], P('section', 'ctx', 'tp'), may hold values from -6 to 6
Outputs:
- attn_out: bfloat16 [2, 4096, 4096], P('section', 'ctx', 'tp')
- d_text_q: bfloat16 [2, 4096, 4096], P('section', 'ctx', 'tp')
- d_text_k: bfloat16 [2, 4096, 512], P('section', 'ctx', 'tp')
- d_text_v: bfloat16 [2, 4096, 512], P('section', 'ctx', 'tp')
- d_frames: bfloat16 [2, 2048, 1280], P('section', 'ctx', 'tp')
- d_proj_w: float32 [1280, 1024], P(('section', 'ctx'), 'tp')
The draws below stay inside these ranges and needn't reach their ends.
Inputs may be any that keep to these rules, and one draw needn't show every extreme that they name: `text_q`: text queries of order one. `text_k`: text keys of order one. `frame_count`: every block has at least one live frame token; some block is full. `text_len`: some block's text slots are all live.
All inputs are finite; a program needn't handle non-finite values.
Results may differ from the reference program's by a relative error of at most 0.015.
Values may be sent and summed in bfloat16 or wider, within the bound.
No kernel may reach another device: no remote copies, remote signals or barrier semaphores. Data moves between devices by JAX's collectives and lax.ppermute only.
A program may use at most 64 MiB of HBM per device.

```python
import jax
import jax.numpy as jnp
from jax import lax

D_VIT = 1280
QHEADS = 32
KVHEADS = 4
HEAD = 128
FR_DEV = 64
TX_DEV = 128
MB = 2
FRAMES = 2048
TEXT = 4096
N_CTX = 32


def draw_text_q(key, part):
    key = jax.random.fold_in(key, 11)
    shape = (MB, N_CTX, TX_DEV, QHEADS, HEAD)
    base = jnp.clip(jax.random.normal(key, shape, jnp.float32), -6.0, 6.0)
    return base.reshape(MB, TEXT, QHEADS * HEAD).astype(jnp.bfloat16)


def draw_text_k(key, part):
    key = jax.random.fold_in(key, 12)
    shape = (MB, N_CTX, TX_DEV, KVHEADS, HEAD)
    base = jnp.clip(jax.random.normal(key, shape, jnp.float32), -6.0, 6.0)
    return base.reshape(MB, TEXT, KVHEADS * HEAD).astype(jnp.bfloat16)


def ragged_counts(key, lowest, highest):
    key_one, key_two = jax.random.split(key)
    total = MB * N_CTX
    counts = jax.random.randint(key_one, (total,), lowest, highest + 1, dtype=jnp.int32)
    position = jax.random.randint(key_two, (), 0, total, dtype=jnp.int32)
    counts = counts.at[position].set(highest)
    counts = counts.at[(position + 1) % total].set(lowest)
    return counts.reshape(MB, N_CTX)


def draw_frame_count(key, part):
    key = jax.random.fold_in(key, 21)
    return ragged_counts(key, max(1, FR_DEV // 4), FR_DEV)


def draw_text_len(key, part):
    key = jax.random.fold_in(key, 22)
    return ragged_counts(key, max(8, TX_DEV // 4), TX_DEV)


def spiked(drawn, own_key, source, target, parts, factor):
    owner, partner = [(jnp.arange(drawn.shape[dim]) // (drawn.shape[dim] // parts)).reshape([-1 if axis == dim else 1 for axis in range(drawn.ndim)]) for dim in (source, target)]
    chosen = jax.random.permutation(own_key, parts)[partner]
    strong = (owner == chosen) | (owner == (partner + parts // 2) % parts)
    return jnp.where(strong, factor * drawn, drawn)


def block_levels(own_key, extent, cuts, least, high):
    loudness = 1.0
    for dim, blocks in cuts:
        heights = jax.random.uniform(jax.random.fold_in(jax.random.fold_in(own_key, 6), dim), (blocks,), jnp.float32, least / len(cuts), high / len(cuts))
        loudness = loudness * jnp.repeat(jnp.exp(heights), extent[dim] // blocks).reshape((-1,) + (1,) * (len(extent) - 1 - dim))
    return loudness


def centred(rng, shape, scale, bound, pieces=(), kind=jnp.bfloat16):
    values = scale * jax.random.normal(rng, shape, jnp.float32)
    if pieces:
        values = values * block_levels(rng, shape, pieces, -0.22, 0.18)
    return jnp.clip(values, -bound, bound).astype(kind)


def bell_draw_with(key, shape, scale, reach, cuts, heavy, kind=jnp.bfloat16):
    entries = scale * jax.random.normal(key, shape, jnp.float32)
    if cuts:
        entries = entries * block_levels(key, shape, cuts, -0.22, 0.18)
    return jnp.clip(spiked(entries, jax.random.fold_in(key, 3), *heavy), -reach, reach).astype(kind)


def setup_inputs(seed: int = 0) -> dict:
    arg_keys = jax.random.split(jax.random.key(seed), 9)
    return {
        "frames": bell_draw_with(arg_keys[0], (MB, FRAMES, D_VIT), 1.0, 6.0, ((0, 2), (1, 32)), (1, 2, 32, 2.75)),
        "proj_w": centred(arg_keys[1], (D_VIT, 2 * KVHEADS * HEAD), D_VIT ** -0.5, 0.15625, ((0, 64), (1, 4))),
        "text_q": draw_text_q(jax.random.fold_in(arg_keys[8], 71), 0),
        "text_k": draw_text_k(jax.random.fold_in(arg_keys[8], 71), 0),
        "text_v": centred(arg_keys[4], (MB, TEXT, KVHEADS * HEAD), 1.0, 6.0, ((0, 2), (1, 32), (2, 4))),
        "frame_count": draw_frame_count(jax.random.fold_in(arg_keys[8], 71), 0),
        "text_len": draw_text_len(jax.random.fold_in(arg_keys[8], 71), 0),
        "grad_out": centred(arg_keys[7], (MB, TEXT, QHEADS * HEAD), 1.0, 6.0, ((0, 2), (1, 32), (2, 4))),
    }


NEGATIVE = -1.0e30


def attend_head(queries, keys, values, grad_rows, allowed, live, score_scale):
    scores = jnp.dot(queries, keys.T, preferred_element_type=jnp.float32) * score_scale
    masked = jnp.where(allowed, scores, NEGATIVE)
    row_max = jnp.max(masked, axis=1, keepdims=True)
    weights = jnp.where(allowed, jnp.exp(masked - row_max), 0.0)
    soft = weights / jnp.sum(weights, axis=1, keepdims=True)
    soft_bf = soft.astype(jnp.bfloat16)
    attended = jnp.dot(soft_bf, values, preferred_element_type=jnp.float32)
    upstream = grad_rows * live[:, None].astype(jnp.bfloat16)
    grad_values = jnp.dot(soft_bf.T, upstream, preferred_element_type=jnp.float32)
    grad_soft = jnp.dot(upstream, values.T, preferred_element_type=jnp.float32)
    row_delta = jnp.sum(upstream.astype(jnp.float32) * attended, axis=1, keepdims=True)
    grad_scores = (soft * (grad_soft - row_delta) * score_scale).astype(jnp.bfloat16)
    grad_queries = jnp.dot(grad_scores, keys, preferred_element_type=jnp.float32).astype(jnp.bfloat16)
    grad_keys = jnp.dot(grad_scores.T, queries, preferred_element_type=jnp.float32)
    output = (attended * live[:, None].astype(jnp.float32)).astype(jnp.bfloat16)
    return output, grad_queries, grad_keys, grad_values


def reference(frames, proj_w, text_q, text_k, text_v, frame_count, text_len, grad_out):
    score_scale = 1.0 / (HEAD ** 0.5)
    group_size = QHEADS // KVHEADS
    block_rows = FR_DEV + TX_DEV
    key_total = N_CTX * block_rows
    query_total = N_CTX * TX_DEV
    frames_flat = frames.reshape(MB * FRAMES, D_VIT)
    visual_kv = jnp.dot(frames_flat, proj_w, preferred_element_type=jnp.float32).astype(jnp.bfloat16)
    visual_kv = visual_kv.reshape(MB, N_CTX, FR_DEV, KVHEADS, 2, HEAD)
    text_keys = text_k.reshape(MB, N_CTX, TX_DEV, KVHEADS, HEAD)
    text_values = text_v.reshape(MB, N_CTX, TX_DEV, KVHEADS, HEAD)
    keys = jnp.concatenate([visual_kv[:, :, :, :, 0, :], text_keys], axis=2).reshape(MB, key_total, KVHEADS, HEAD)
    values = jnp.concatenate([visual_kv[:, :, :, :, 1, :], text_values], axis=2).reshape(MB, key_total, KVHEADS, HEAD)
    frame_slot = jnp.arange(FR_DEV, dtype=jnp.int32)
    text_slot = jnp.arange(TX_DEV, dtype=jnp.int32)
    key_live = jnp.concatenate([frame_slot[None, None, :] < frame_count[:, :, None],
                                text_slot[None, None, :] < text_len[:, :, None]], axis=2).reshape(MB, key_total)
    query_live = (text_slot[None, None, :] < text_len[:, :, None]).reshape(MB, query_total)
    key_order = jnp.arange(key_total, dtype=jnp.int32)
    query_order = (jnp.arange(N_CTX, dtype=jnp.int32)[:, None] * block_rows + FR_DEV + text_slot[None, :]).reshape(-1)
    causal = key_order[None, :] <= query_order[:, None]
    query_heads = text_q.reshape(MB, query_total, QHEADS, HEAD)
    grad_heads = grad_out.reshape(MB, query_total, QHEADS, HEAD)

    def one_head(head_index):
        batch_index = head_index // QHEADS
        query_head = head_index % QHEADS
        kv_head = query_head // group_size
        allowed = causal & key_live[batch_index][None, :]
        return attend_head(query_heads[batch_index, :, query_head], keys[batch_index, :, kv_head],
                           values[batch_index, :, kv_head], grad_heads[batch_index, :, query_head],
                           allowed, query_live[batch_index], score_scale)

    outputs, grad_queries, grad_keys, grad_values = lax.map(one_head, jnp.arange(MB * QHEADS, dtype=jnp.int32))
    attn_out = outputs.reshape(MB, QHEADS, query_total, HEAD).transpose(0, 2, 1, 3).reshape(MB, query_total, QHEADS * HEAD)
    d_text_q = grad_queries.reshape(MB, QHEADS, query_total, HEAD).transpose(0, 2, 1, 3).reshape(MB, query_total, QHEADS * HEAD)
    key_grad = grad_keys.reshape(MB, KVHEADS, group_size, key_total, HEAD).sum(axis=2)
    value_grad = grad_values.reshape(MB, KVHEADS, group_size, key_total, HEAD).sum(axis=2)
    key_grad = key_grad.transpose(0, 2, 1, 3).reshape(MB, N_CTX, block_rows, KVHEADS, HEAD)
    value_grad = value_grad.transpose(0, 2, 1, 3).reshape(MB, N_CTX, block_rows, KVHEADS, HEAD)
    d_text_k = key_grad[:, :, FR_DEV:].reshape(MB, query_total, KVHEADS * HEAD).astype(jnp.bfloat16)
    d_text_v = value_grad[:, :, FR_DEV:].reshape(MB, query_total, KVHEADS * HEAD).astype(jnp.bfloat16)
    visual_grad = jnp.stack([key_grad[:, :, :FR_DEV], value_grad[:, :, :FR_DEV]], axis=4)
    visual_grad = visual_grad.reshape(MB * FRAMES, 2 * KVHEADS * HEAD).astype(jnp.bfloat16)
    d_proj_w = jnp.dot(frames_flat.T, visual_grad, preferred_element_type=jnp.float32)
    d_frames = jnp.dot(visual_grad, proj_w.T, preferred_element_type=jnp.float32).astype(jnp.bfloat16)
    d_frames = d_frames.reshape(MB, FRAMES, D_VIT)
    return attn_out, d_text_q, d_text_k, d_text_v, d_frames, d_proj_w
```

```python
import functools
import math

import jax
import jax.numpy as jnp
from jax import lax
from jax.experimental import pallas as pl
from jax.experimental.pallas import tpu as pltpu
from jax.sharding import PartitionSpec as P

HEAD = 128
INNER = 4
LANES = 256
STAT_ROWS = 144
NEGATIVE = -1e30
DEAD_VALUE = 1e30
DEAD_BOUND = 1e29
VMEM_BYTES = 48 * 1024 * 1024
F32 = jnp.float32
BF16 = jnp.bfloat16


def dot(left, right):
    return jnp.dot(left, right, preferred_element_type=F32)


def turned(block):
    return block.astype(F32).T.astype(BF16)


def values_with_ones(values):
    rows = values.shape[0]
    return jnp.concatenate([turned(values), jnp.ones((STAT_ROWS - HEAD, rows), BF16)], axis=0)


def own_kernel(exp_scale, len_ref, q_ref, grad_ref, kv_ref, qt_ref, qr_ref, gt_ref, p_ref, m_ref, ot_ref):
    tokens = q_ref.shape[0]
    heads = q_ref.shape[1] // HEAD
    length = len_ref[0, 0]
    live = lax.broadcasted_iota(jnp.int32, (tokens, HEAD), 0) < length
    values = values_with_ones(kv_ref[:, HEAD:])
    key_row = lax.broadcasted_iota(jnp.int32, (tokens, tokens), 0)
    query_row = lax.broadcasted_iota(jnp.int32, (tokens, tokens), 1)
    allowed = (key_row <= query_row) & (key_row < length)
    for head in range(heads):
        span = slice(head * HEAD, (head + 1) * HEAD)
        place = slice(head * tokens, (head + 1) * tokens)
        queries = q_ref[:, span]
        queries_t = turned(queries)
        qr_ref[place, :] = queries
        qt_ref[:, place] = queries_t
        gt_ref[:, place] = jnp.where(live, grad_ref[:, span].astype(F32), 0.0).T.astype(BF16)
        scores = jnp.where(allowed, dot(kv_ref[:, :HEAD], queries_t) * exp_scale, NEGATIVE)
        top = jnp.max(scores, axis=0, keepdims=True)
        weights = jnp.exp2(scores - top).astype(BF16)
        p_ref[0, :, place] = weights
        m_ref[0, :, place] = top
        ot_ref[:, place] = dot(values, weights)


def forward_kernel(exp_scale, slots, lim_ref, kv_ref, qt_ref, m0_ref, ot0_ref, p_ref, mc_ref, m_ref, ot_ref):
    part = pl.program_id(0)
    rows = kv_ref.shape[1]

    @pl.when(part == 0)
    def _():
        m_ref[...] = m0_ref[...]
        ot_ref[...] = ot0_ref[...]

    keys = kv_ref[0, :, :HEAD]
    row_values = kv_ref[0, :, HEAD:]
    values = values_with_ones(row_values)
    block = (lax.broadcasted_iota(jnp.int32, (rows, HEAD), 0) // slots) * INNER + part
    dead = (row_values.astype(F32) > DEAD_BOUND) | (block >= lim_ref[0, 0])
    bias = jnp.where(dead, NEGATIVE, 0.0)
    bias = jnp.concatenate([bias] * (LANES // HEAD), axis=1)
    for tile in range(qt_ref.shape[1] // LANES):
        place = slice(tile * LANES, (tile + 1) * LANES)
        scores = dot(keys, qt_ref[:, place]) * exp_scale + bias
        before = m_ref[0, :, place]
        top = jnp.maximum(before, jnp.max(scores, axis=0, keepdims=True))
        weights = jnp.exp2(scores - top).astype(BF16)
        p_ref[0, :, place] = weights
        mc_ref[0, :, place] = top
        m_ref[0, :, place] = top
        ot_ref[:, place] = ot_ref[:, place] * jnp.exp2(before - top) + dot(values, weights)


def middle_kernel(len_ref, ot_ref, gt_ref, out_ref, inv_ref, delta_ref):
    tokens = out_ref.shape[0]
    heads = out_ref.shape[1] // HEAD
    live = lax.broadcasted_iota(jnp.int32, (tokens, HEAD), 0) < len_ref[0, 0]
    for head in range(heads):
        span = slice(head * HEAD, (head + 1) * HEAD)
        place = slice(head * tokens, (head + 1) * tokens)
        inverse = 1.0 / ot_ref[HEAD : HEAD + 1, place]
        attended = ot_ref[:HEAD, place] * inverse
        out_ref[:, span] = jnp.where(live, attended.T, 0.0).astype(BF16)
        inv_ref[0, :, place] = inverse
        delta_ref[0, :, place] = jnp.sum(gt_ref[:, place].astype(F32) * attended, axis=0, keepdims=True)


def backward_kernel(scale, kv_ref, p_ref, mc_ref, m_ref, inv_ref, delta_ref, gt_ref, qr_ref, dq0_ref, dkv_ref, dq_ref, gt_now, gr_now, ds_now):
    @pl.when(pl.program_id(0) == 0)
    def _():
        dq_ref[...] = dq0_ref[...]

    keys_t = turned(kv_ref[0, :, :HEAD])
    values = kv_ref[0, :, HEAD:]
    width = qr_ref.shape[0]
    factor = jnp.exp2(mc_ref[0] - m_ref[0]) * inv_ref[0]
    shift = delta_ref[0] * factor
    for start in range(0, width, HEAD):
        place = slice(start, start + HEAD)
        scaled = gt_ref[:, place].astype(F32) * factor[:, place]
        gt_now[:, place] = scaled.astype(BF16)
        gr_now[place, :] = scaled.T.astype(BF16)
    for start in range(0, width, LANES):
        place = slice(start, start + LANES)
        grad_soft = dot(values, gt_now[:, place])
        grad_scores = (p_ref[0, :, place].astype(F32) * (grad_soft - shift[:, place])).astype(BF16)
        ds_now[:, place] = grad_scores
        dq_ref[:, place] = dq_ref[:, place] + dot(keys_t, grad_scores)
    dkv_ref[0, :, HEAD:] = dot(p_ref[0], gr_now[...]).astype(dkv_ref.dtype)
    dkv_ref[0, :, :HEAD] = (dot(ds_now[...], qr_ref[...]) * scale).astype(dkv_ref.dtype)


def whole(array):
    zeros = (0,) * array.ndim
    return pl.BlockSpec(array.shape, lambda *_: zeros)


def by_part(shape):
    return pl.BlockSpec((1,) + shape[1:], lambda part: (part, 0, 0))


def scalar_spec():
    return pl.BlockSpec(memory_space=pltpu.SMEM)


def params():
    return pltpu.CompilerParams(vmem_limit_bytes=VMEM_BYTES)


def shape_of(shape, dtype):
    return jax.ShapeDtypeStruct(shape, dtype)


def own_call(length, queries, grads, kv):
    tokens, width = queries.shape
    columns = tokens * (width // HEAD)
    outs = [
        shape_of((HEAD, columns), BF16),
        shape_of((columns, HEAD), BF16),
        shape_of((HEAD, columns), BF16),
        shape_of((1, tokens, columns), BF16),
        shape_of((1, 1, columns), F32),
        shape_of((STAT_ROWS, columns), F32),
    ]
    return pl.pallas_call(
        functools.partial(own_kernel, math.log2(math.e) / math.sqrt(HEAD)),
        grid=(1,),
        out_shape=outs,
        in_specs=[scalar_spec(), whole(queries), whole(grads), whole(kv)],
        out_specs=[whole(item) for item in outs],
        compiler_params=params(),
        cost_estimate=pl.CostEstimate(
            flops=4 * tokens * columns * HEAD, bytes_accessed=3_000_000, transcendentals=tokens * columns
        ),
    )(length, queries, grads, kv)


def forward_call(limit, kv, slots, queries_t, top, out_t):
    parts, rows, _ = kv.shape
    columns = queries_t.shape[1]
    outs = [
        shape_of((parts, rows, columns), BF16),
        shape_of((parts, 1, columns), F32),
        shape_of(top.shape, F32),
        shape_of(out_t.shape, F32),
    ]
    return pl.pallas_call(
        functools.partial(forward_kernel, math.log2(math.e) / math.sqrt(HEAD), slots),
        grid=(parts,),
        out_shape=outs,
        in_specs=[scalar_spec(), by_part(kv.shape), whole(queries_t), whole(top), whole(out_t)],
        out_specs=[by_part(outs[0].shape), by_part(outs[1].shape), whole(outs[2]), whole(outs[3])],
        compiler_params=params(),
        cost_estimate=pl.CostEstimate(
            flops=8 * parts * rows * columns * HEAD,
            bytes_accessed=2 * parts * rows * (columns + 256),
            transcendentals=parts * rows * columns,
        ),
    )(limit, kv, queries_t, top, out_t)


def middle_call(length, out_t, grads_t, tokens):
    columns = out_t.shape[1]
    outs = [
        shape_of((tokens, columns // tokens * HEAD), BF16),
        shape_of((1, 1, columns), F32),
        shape_of((1, 1, columns), F32),
    ]
    return pl.pallas_call(
        middle_kernel,
        grid=(1,),
        out_shape=outs,
        in_specs=[scalar_spec(), whole(out_t), whole(grads_t)],
        out_specs=[whole(item) for item in outs],
        compiler_params=params(),
        cost_estimate=pl.CostEstimate(flops=columns * HEAD * 4, bytes_accessed=2_000_000, transcendentals=0),
    )(length, out_t, grads_t)


def backward_call(kv, weights, tops, top, inverse, delta, grads_t, queries, dq_t, dtype):
    parts, rows, width = kv.shape
    columns = queries.shape[0]
    outs = [shape_of((parts, rows, width), dtype), shape_of(dq_t.shape, F32)]
    return pl.pallas_call(
        functools.partial(backward_kernel, 1.0 / math.sqrt(HEAD)),
        grid=(parts,),
        out_shape=outs,
        in_specs=[
            by_part(kv.shape),
            by_part(weights.shape),
            by_part(tops.shape),
            whole(top),
            whole(inverse),
            whole(delta),
            whole(grads_t),
            whole(queries),
            whole(dq_t),
        ],
        out_specs=[by_part(outs[0].shape), whole(outs[1])],
        scratch_shapes=[
            pltpu.VMEM((HEAD, columns), BF16),
            pltpu.VMEM((columns, HEAD), BF16),
            pltpu.VMEM((rows, columns), BF16),
        ],
        compiler_params=params(),
        cost_estimate=pl.CostEstimate(
            flops=16 * parts * rows * columns * HEAD,
            bytes_accessed=2 * parts * rows * (columns + 512),
            transcendentals=0,
        ),
    )(kv, weights, tops, top, inverse, delta, grads_t, queries, dq_t)


def per_device(frames, proj_w, text_q, text_k, text_v, frame_count, text_len, grad_out):
    frame_rows = frames.shape[1]
    text_rows = text_q.shape[1]
    ctx_size = lax.axis_size("ctx")
    outer = ctx_size // INNER
    my_index = lax.axis_index("ctx")
    inner_groups = [[o * INNER + i for i in range(INNER)] for o in range(outer)]
    outer_groups = [[o * INNER + i for o in range(outer)] for i in range(INNER)]

    def exchange(array, groups):
        return lax.all_to_all(
            array, "ctx", split_axis=0, concat_axis=0, tiled=True, axis_index_groups=groups
        )

    def spread(block):
        rows = block.shape[0]
        column = exchange(jnp.broadcast_to(block[None], (outer,) + block.shape), outer_groups)
        column = column.reshape(1, outer * rows, -1)
        return exchange(jnp.broadcast_to(column, (INNER,) + column.shape[1:]), inner_groups)

    def gathered_sum(parts):
        across = exchange(parts, inner_groups).astype(F32).sum(axis=0).astype(BF16)
        across = across.reshape(outer, -1, across.shape[-1])
        return exchange(across, outer_groups).astype(F32).sum(axis=0)

    def marked(values, count):
        slot = lax.broadcasted_iota(jnp.int32, values.shape, 0)
        return jnp.where(slot < count, values, jnp.asarray(DEAD_VALUE, BF16))

    features = frames[0]
    text_kv = jnp.concatenate([text_k[0], marked(text_v[0], text_len[0, 0])], axis=1)
    all_axes = lax.axis_size("section") * ctx_size
    weights = lax.all_to_all(
        jnp.broadcast_to(proj_w[None], (all_axes,) + proj_w.shape),
        ("section", "ctx"), split_axis=0, concat_axis=0, tiled=True,
    ).reshape(-1, proj_w.shape[1])
    text_all = spread(text_kv)
    visual = dot(features, weights).astype(BF16)
    visual = jnp.concatenate([visual[:, :HEAD], marked(visual[:, HEAD:], frame_count[0, 0])], axis=1)
    visual_all = spread(visual)

    limit = my_index.astype(jnp.int32).reshape(1, 1)
    queries_t, queries, grads_t, p_own, m_own, out_t = own_call(text_len, text_q[0], grad_out[0], text_kv)
    p_text, m_text, top, out_t = forward_call(limit, text_all, text_rows, queries_t, m_own, out_t)
    p_vis, m_vis, top, out_t = forward_call(limit + 1, visual_all, frame_rows, queries_t, top, out_t)
    attn_out, inverse, delta = middle_call(text_len, out_t, grads_t, text_rows)
    dq_t = jnp.zeros((HEAD, queries.shape[0]), F32)
    common = (top, inverse, delta, grads_t, queries)
    dkv_vis, dq_t = backward_call(visual_all, p_vis, m_vis, *common, dq_t, BF16)
    dkv_own, dq_t = backward_call(text_kv[None], p_own, m_own, *common, dq_t, F32)
    dkv_text, dq_t = backward_call(text_all, p_text, m_text, *common, dq_t, BF16)
    visual_grad = gathered_sum(dkv_vis).astype(BF16)
    text_grad = (gathered_sum(dkv_text) + dkv_own[0]).astype(BF16)
    d_text_q = (dq_t * (1.0 / math.sqrt(HEAD))).reshape(HEAD, -1, text_rows).transpose(2, 1, 0)
    d_text_q = d_text_q.astype(BF16).reshape(1, text_rows, -1)

    proj_terms = dot(features.T, visual_grad).astype(BF16)
    proj_terms = proj_terms.reshape((all_axes,) + proj_w.shape)
    d_proj_w = lax.all_to_all(
        proj_terms, ("section", "ctx"), split_axis=0, concat_axis=0, tiled=True
    ).astype(F32).sum(axis=0)
    tp_size = lax.axis_size("tp")
    frame_terms = lax.dot_general(
        visual_grad, weights.reshape(tp_size, -1, weights.shape[1]), (((1,), (2,)), ((), ())),
        preferred_element_type=F32,
    ).astype(BF16).transpose(1, 0, 2)
    d_frames = lax.all_to_all(frame_terms, "tp", split_axis=0, concat_axis=0, tiled=True)
    d_frames = d_frames.astype(F32).sum(axis=0).astype(BF16)[None]
    return (attn_out[None], d_text_q, text_grad[None, :, :HEAD], text_grad[None, :, HEAD:], d_frames, d_proj_w)


def solution(mesh):
    in_specs = (
        P("section", "ctx", None),
        P(("section", "ctx"), "tp"),
        P("section", "ctx", "tp"),
        P("section", "ctx", "tp"),
        P("section", "ctx", "tp"),
        P("section", "ctx"),
        P("section", "ctx"),
        P("section", "ctx", "tp"),
    )
    out_specs = (
        P("section", "ctx", "tp"),
        P("section", "ctx", "tp"),
        P("section", "ctx", "tp"),
        P("section", "ctx", "tp"),
        P("section", "ctx", "tp"),
        P(("section", "ctx"), "tp"),
    )
    return jax.shard_map(
        per_device, mesh=mesh, in_specs=in_specs, out_specs=out_specs, check_vma=False
    )
```

```python
import functools
import math

import jax
import jax.numpy as jnp
from jax import lax
from jax.experimental import pallas as pl
from jax.experimental.pallas import tpu as pltpu
from jax.sharding import PartitionSpec as P

HEAD = 128
INNER = 4
LANES = 256
KEY_ROWS = 256
STAT_ROWS = 144
NEGATIVE = -1e30
DEAD_VALUE = 1e30
DEAD_BOUND = 1e29
VMEM_BYTES = 16 * 1024 * 1024
F32 = jnp.float32
BF16 = jnp.bfloat16


def dot(left, right):
    return jnp.dot(left, right, preferred_element_type=F32)


def turned(block):
    return block.astype(F32).T.astype(BF16)


def values_with_ones(values):
    rows = values.shape[0]
    return jnp.concatenate([turned(values), jnp.ones((STAT_ROWS - HEAD, rows), BF16)], axis=0)


def own_kernel(exp_scale, len_ref, q_ref, grad_ref, kv_ref, qt_ref, qr_ref, gt_ref, p_ref, m_ref, ot_ref):
    tokens = q_ref.shape[0]
    heads = q_ref.shape[1] // HEAD
    length = len_ref[0, 0]
    live = lax.broadcasted_iota(jnp.int32, (tokens, HEAD), 0) < length
    values = values_with_ones(kv_ref[:, HEAD:])
    key_row = lax.broadcasted_iota(jnp.int32, (tokens, tokens), 0)
    query_row = lax.broadcasted_iota(jnp.int32, (tokens, tokens), 1)
    allowed = (key_row <= query_row) & (key_row < length)
    for head in range(heads):
        span = slice(head * HEAD, (head + 1) * HEAD)
        place = slice(head * tokens, (head + 1) * tokens)
        queries = q_ref[:, span]
        queries_t = turned(queries)
        qr_ref[place, :] = queries
        qt_ref[:, place] = queries_t
        gt_ref[:, place] = jnp.where(live, grad_ref[:, span].astype(F32), 0.0).T.astype(BF16)
        scores = jnp.where(allowed, dot(kv_ref[:, :HEAD], queries_t) * exp_scale, NEGATIVE)
        top = jnp.max(scores, axis=0, keepdims=True)
        weights = jnp.exp(scores - top).astype(BF16)
        p_ref[:, place] = weights
        m_ref[:, place] = top
        ot_ref[:, place] = dot(values, weights)


def forward_kernel(exp_scale, slots, lim_ref, kv_ref, qt_ref, m0_ref, ot0_ref, p_ref, m_ref, ot_ref, s_now):
    rows = kv_ref.shape[0]
    width = qt_ref.shape[1]
    row_values = kv_ref[:, HEAD:]
    values = values_with_ones(row_values)
    block = (lax.broadcasted_iota(jnp.int32, (rows, HEAD), 0) // slots) * INNER + lim_ref[0, 1]
    dead = (row_values.astype(F32) > DEAD_BOUND) | (block >= lim_ref[0, 0])
    bias = jnp.where(dead, NEGATIVE, 0.0)
    peak = jnp.full((8, width), NEGATIVE, F32)
    for start in range(0, rows, KEY_ROWS):
        span = slice(start, start + KEY_ROWS)
        wide = jnp.concatenate([bias[span]] * (width // HEAD), axis=1)
        scores = dot(kv_ref[span, :HEAD], qt_ref[...]) * exp_scale + wide
        s_now[span, :] = scores
        peak = jnp.maximum(peak, jnp.max(scores.reshape(KEY_ROWS // 8, 8, width), axis=0))
    before = m0_ref[...]
    top = jnp.maximum(before, jnp.max(peak, axis=0, keepdims=True))
    m_ref[...] = top
    total = ot0_ref[...] * jnp.exp(before - top)
    for start in range(0, rows, KEY_ROWS):
        span = slice(start, start + KEY_ROWS)
        weights = jnp.exp(s_now[span, :] - top).astype(BF16)
        p_ref[span, :] = weights
        total = total + dot(values[:, span], weights)
    ot_ref[...] = total


def middle_kernel(len_ref, ot_ref, gt_ref, out_ref, inv_ref, delta_ref):
    tokens = out_ref.shape[0]
    heads = out_ref.shape[1] // HEAD
    live = lax.broadcasted_iota(jnp.int32, (tokens, HEAD), 0) < len_ref[0, 0]
    for head in range(heads):
        span = slice(head * HEAD, (head + 1) * HEAD)
        place = slice(head * tokens, (head + 1) * tokens)
        inverse = 1.0 / ot_ref[HEAD : HEAD + 1, place]
        attended = ot_ref[:HEAD, place] * inverse
        out_ref[:, span] = jnp.where(live, attended.T, 0.0).astype(BF16)
        inv_ref[:, place] = inverse
        delta_ref[:, place] = jnp.sum(gt_ref[:, place].astype(F32) * attended, axis=0, keepdims=True)


def backward_kernel(scale, kv_ref, p_ref, mc_ref, m_ref, inv_ref, delta_ref, gt_ref, qr_ref, dq0_ref, dkv_ref, dq_ref, gt_now, gr_now, ds_now):
    keys_t = turned(kv_ref[:, :HEAD])
    values = kv_ref[:, HEAD:]
    width = qr_ref.shape[0]
    factor = jnp.exp(mc_ref[...] - m_ref[...]) * inv_ref[...]
    shift = delta_ref[...] * factor
    for start in range(0, width, HEAD):
        place = slice(start, start + HEAD)
        scaled = gt_ref[:, place].astype(F32) * factor[:, place]
        gt_now[:, place] = scaled.astype(BF16)
        gr_now[place, :] = scaled.T.astype(BF16)
    for start in range(0, width, LANES):
        place = slice(start, start + LANES)
        grad_soft = dot(values, gt_now[:, place])
        grad_scores = (p_ref[:, place].astype(F32) * (grad_soft - shift[:, place])).astype(BF16)
        ds_now[:, place] = grad_scores
        dq_ref[:, place] = dq0_ref[:, place] + dot(keys_t, grad_scores)
    dkv_ref[:, HEAD:] = dot(p_ref[...], gr_now[...]).astype(dkv_ref.dtype)
    dkv_ref[:, :HEAD] = (dot(ds_now[...], qr_ref[...]) * scale).astype(dkv_ref.dtype)


def whole(array):
    zeros = (0,) * array.ndim
    return pl.BlockSpec(array.shape, lambda *_: zeros)


def scalar_spec():
    return pl.BlockSpec(memory_space=pltpu.SMEM)


def params():
    return pltpu.CompilerParams(vmem_limit_bytes=VMEM_BYTES)


def shape_of(shape, dtype):
    return jax.ShapeDtypeStruct(shape, dtype)


def own_call(length, queries, grads, kv):
    tokens, width = queries.shape
    columns = tokens * (width // HEAD)
    outs = [
        shape_of((HEAD, columns), BF16),
        shape_of((columns, HEAD), BF16),
        shape_of((HEAD, columns), BF16),
        shape_of((tokens, columns), BF16),
        shape_of((1, columns), F32),
        shape_of((STAT_ROWS, columns), F32),
    ]
    return pl.pallas_call(
        functools.partial(own_kernel, 1.0 / math.sqrt(HEAD)),
        grid=(1,),
        out_shape=outs,
        in_specs=[scalar_spec(), whole(queries), whole(grads), whole(kv)],
        out_specs=[whole(item) for item in outs],
        compiler_params=params(),
        cost_estimate=pl.CostEstimate(
            flops=4 * tokens * columns * HEAD, bytes_accessed=3_000_000, transcendentals=tokens * columns
        ),
    )(length, queries, grads, kv)


def forward_call(place, kv, slots, queries_t, top, out_t):
    rows = kv.shape[0]
    columns = queries_t.shape[1]
    outs = [shape_of((rows, columns), BF16), shape_of(top.shape, F32), shape_of(out_t.shape, F32)]
    return pl.pallas_call(
        functools.partial(forward_kernel, 1.0 / math.sqrt(HEAD), slots),
        grid=(1,),
        out_shape=outs,
        in_specs=[scalar_spec(), whole(kv), whole(queries_t), whole(top), whole(out_t)],
        out_specs=[whole(item) for item in outs],
        scratch_shapes=[pltpu.VMEM((rows, columns), F32)],
        compiler_params=params(),
        cost_estimate=pl.CostEstimate(
            flops=20 * rows * columns * HEAD,
            bytes_accessed=2 * rows * (columns + 256),
            transcendentals=rows * columns,
        ),
    )(place, kv, queries_t, top, out_t)


def middle_call(length, out_t, grads_t, tokens):
    columns = out_t.shape[1]
    outs = [
        shape_of((tokens, columns // tokens * HEAD), BF16),
        shape_of((1, columns), F32),
        shape_of((1, columns), F32),
    ]
    return pl.pallas_call(
        middle_kernel,
        grid=(1,),
        out_shape=outs,
        in_specs=[scalar_spec(), whole(out_t), whole(grads_t)],
        out_specs=[whole(item) for item in outs],
        compiler_params=params(),
        cost_estimate=pl.CostEstimate(flops=columns * HEAD * 4, bytes_accessed=2_000_000, transcendentals=0),
    )(length, out_t, grads_t)


def backward_call(kv, weights, tops, top, inverse, delta, grads_t, queries, dq_t, dtype):
    rows, width = kv.shape
    columns = queries.shape[0]
    operands = (kv, weights, tops, top, inverse, delta, grads_t, queries, dq_t)
    outs = [shape_of((rows, width), dtype), shape_of(dq_t.shape, F32)]
    return pl.pallas_call(
        functools.partial(backward_kernel, 1.0 / math.sqrt(HEAD)),
        grid=(1,),
        out_shape=outs,
        in_specs=[whole(item) for item in operands],
        out_specs=[whole(item) for item in outs],
        scratch_shapes=[
            pltpu.VMEM((HEAD, columns), BF16),
            pltpu.VMEM((columns, HEAD), BF16),
            pltpu.VMEM((rows, columns), BF16),
        ],
        compiler_params=params(),
        cost_estimate=pl.CostEstimate(
            flops=32 * rows * columns * HEAD,
            bytes_accessed=2 * rows * (columns + 512),
            transcendentals=0,
        ),
    )(*operands)


def per_device(frames, proj_w, text_q, text_k, text_v, frame_count, text_len, grad_out):
    frame_rows = frames.shape[1]
    text_rows = text_q.shape[1]
    proj_rows = proj_w.shape[0]
    ctx_size = lax.axis_size("ctx")
    sections = lax.axis_size("section")
    outer = ctx_size // INNER
    my_index = lax.axis_index("ctx")
    my_inner = my_index % INNER
    my_section = lax.axis_index("section")
    outer_groups = [[o * INNER + i for o in range(outer)] for i in range(INNER)]
    shifts = (2, 1, INNER - 1)
    sources = [my_inner] + [(my_inner + INNER - shift) % INNER for shift in shifts]

    def along_outer(array):
        return lax.all_to_all(
            array, "ctx", split_axis=0, concat_axis=0, tiled=True, axis_index_groups=outer_groups
        )

    def along_inner(array, shift):
        pairs = [
            (o * INNER + i, o * INNER + (i + shift) % INNER) for o in range(outer) for i in range(INNER)
        ]
        return lax.ppermute(array, "ctx", pairs)

    def across_sections(array):
        return lax.ppermute(array, "section", [(i, sections - 1 - i) for i in range(sections)])

    def copies(block):
        return jnp.broadcast_to(block[None], (outer,) + block.shape)

    def inner_spread(block):
        return [block] + [along_inner(block, shift) for shift in shifts]

    def inner_sum(parts):
        moved = [parts[0]] + [along_inner(part, INNER - shift) for part, shift in zip(parts[1:], shifts)]
        return sum(part.astype(F32) for part in moved)

    def outer_sum(total):
        return along_outer(total.astype(BF16)).astype(F32).sum(axis=0)

    def marked(values, count):
        slot = lax.broadcasted_iota(jnp.int32, values.shape, 0)
        return jnp.where(slot < count, values, jnp.asarray(DEAD_VALUE, BF16))

    def tied(values, *others):
        return lax.optimization_barrier((values,) + others)[0]

    features = frames[0]
    slices = features.reshape(frame_rows, sections, outer, INNER, proj_rows)
    flipped = lax.rev(slices, (1,))
    slices = jnp.where(my_section == 0, slices, flipped).transpose(3, 0, 2, 1, 4)
    slices = slices.reshape(INNER, frame_rows, outer * sections * proj_rows)

    def feature_slice(inner):
        return lax.dynamic_index_in_dim(slices, inner, 0, False)

    features_now = jnp.concatenate([feature_slice(inner) for inner in sources], axis=1)

    text_kv = jnp.concatenate([text_k[0], marked(text_v[0], text_len[0, 0])], axis=1)
    width = text_kv.shape[1]
    pair_rows = sections * proj_rows
    pair = jnp.concatenate([proj_w, across_sections(proj_w)], axis=0)
    padding = jnp.zeros((-pair_rows % 16, width), BF16)
    first = along_outer(copies(jnp.concatenate([text_kv, pair, padding], axis=0)))
    text_column = first[:, :text_rows].reshape(outer * text_rows, width)
    proj_column = first[:, text_rows : text_rows + pair_rows].reshape(outer * pair_rows, width)
    near = [proj_column]
    inner_features = [feature_slice(my_inner)]
    for shift in shifts:
        sent = feature_slice((my_inner + shift) % INNER).reshape(-1, width)
        moved = along_inner(jnp.concatenate([proj_column, sent], axis=0), shift)
        near.append(moved[: outer * pair_rows])
        inner_features.append(moved[outer * pair_rows :].reshape(frame_rows, -1))
    weights_now = jnp.concatenate(near, axis=0)
    text_parts = [text_column] + inner_spread(tied(text_column, weights_now))[1:]

    queries_t, queries, grads_t, p_own, m_own, out_t = own_call(text_len, text_q[0], grad_out[0], text_kv)

    def forward(part, source, limit, slots, top, out_t):
        place = jnp.stack([limit, source]).astype(jnp.int32).reshape(1, 2)
        weights_t, top, out_t = forward_call(place, part, slots, queries_t, top, out_t)
        return (part, weights_t, top), top, out_t

    kept, top, out_t = forward(text_parts[0], sources[0], my_index, text_rows, m_own, out_t)
    kept_text = [kept]
    visual = dot(tied(features_now, top), weights_now).astype(BF16)
    visual = jnp.concatenate([visual[:, :HEAD], marked(visual[:, HEAD:], frame_count[0, 0])], axis=1)
    visual_column = along_outer(copies(visual)).reshape(outer * frame_rows, width)
    visual_parts = inner_spread(visual_column)

    tp_size = lax.axis_size("tp")
    tp_index = lax.axis_index("tp")
    order = jnp.stack(sources)
    back = jnp.zeros((INNER,), jnp.int32).at[order].set(jnp.arange(INNER, dtype=jnp.int32))
    weights = weights_now.reshape(INNER, outer, sections, proj_rows, width)
    weights = jnp.take(weights, back, axis=0)
    weights = jnp.where(my_section == 0, weights, lax.rev(weights, (2,)))
    weights = weights.transpose(2, 1, 0, 3, 4).reshape(tp_size, -1, width)
    top, weights = lax.optimization_barrier((top, weights))
    for part, source in zip(text_parts[1:], sources[1:]):
        kept, top, out_t = forward(part, source, my_index, text_rows, top, out_t)
        kept_text.append(kept)
    kept_visual = []
    for part, source in zip(visual_parts, sources):
        kept, top, out_t = forward(part, source, my_index + 1, frame_rows, top, out_t)
        kept_visual.append(kept)
    attn_out, inverse, delta = middle_call(text_len, out_t, grads_t, text_rows)
    dq_t = jnp.zeros((HEAD, queries.shape[0]), F32)
    common = (top, inverse, delta, grads_t, queries)

    def backward(kept, dq_t):
        return backward_call(*kept, *common, dq_t, BF16)

    dkv_visual = [None] * INNER
    for index in (1, 2, 3, 0):
        dkv_visual[index], dq_t = backward(kept_visual[index], dq_t)
    dkv_text = [None] * INNER
    for index in (1, 2):
        dkv_text[index], dq_t = backward(kept_text[index], dq_t)
    visual_sum = inner_sum(dkv_visual).reshape(outer, frame_rows, width).astype(BF16)
    dq_t = tied(dq_t, visual_sum)
    for index in (3, 0):
        dkv_text[index], dq_t = backward(kept_text[index], dq_t)
    dkv_own, dq_t = backward_call(text_kv, p_own, m_own, *common, dq_t, F32)
    visual_grad = outer_sum(visual_sum).astype(BF16)
    visual_grad, dkv_text = lax.optimization_barrier((visual_grad, dkv_text))

    proj_terms = dot(jnp.concatenate(inner_features, axis=0).T, jnp.concatenate(inner_spread(visual_grad), axis=0))
    proj_terms = proj_terms.reshape(outer, sections, proj_rows, width)
    proj_terms = proj_terms[:, 0] + across_sections(proj_terms[:, 1].astype(BF16)).astype(F32)
    d_proj_w = outer_sum(proj_terms)

    def frame_part(owner):
        part = lax.dynamic_index_in_dim(weights, owner, 0, False)
        return lax.dot_general(visual_grad, part, (((1,), (1,)), ((), ())), preferred_element_type=F32)

    d_frames = frame_part(tp_index).astype(BF16).astype(F32)
    for flip in range(1, tp_size):
        pairs = [(i, i ^ flip) for i in range(tp_size)]
        d_frames = d_frames + lax.ppermute(frame_part(tp_index ^ flip).astype(BF16), "tp", pairs).astype(F32)
    d_frames = d_frames.astype(BF16)[None]
    text_sum = inner_sum(dkv_text).reshape(outer, text_rows, width)
    text_grad = (outer_sum(tied(text_sum, d_proj_w, d_frames)) + dkv_own).astype(BF16)
    d_text_q = (dq_t * (1.0 / math.sqrt(HEAD))).reshape(HEAD, -1, text_rows).transpose(2, 1, 0)
    d_text_q = d_text_q.astype(BF16).reshape(1, text_rows, -1)

    return (attn_out[None], d_text_q, text_grad[None, :, :HEAD], text_grad[None, :, HEAD:], d_frames, d_proj_w)


def solution(mesh):
    in_specs = (
        P("section", "ctx", None),
        P(("section", "ctx"), "tp"),
        P("section", "ctx", "tp"),
        P("section", "ctx", "tp"),
        P("section", "ctx", "tp"),
        P("section", "ctx"),
        P("section", "ctx"),
        P("section", "ctx", "tp"),
    )
    out_specs = (
        P("section", "ctx", "tp"),
        P("section", "ctx", "tp"),
        P("section", "ctx", "tp"),
        P("section", "ctx", "tp"),
        P("section", "ctx", "tp"),
        P(("section", "ctx"), "tp"),
    )
    return jax.shard_map(
        per_device, mesh=mesh, in_specs=in_specs, out_specs=out_specs, check_vma=False
    )
```

```python
import functools
import math

import jax
import jax.numpy as jnp
from jax import lax
from jax.experimental import pallas as pl
from jax.experimental.pallas import tpu as pltpu
from jax.sharding import PartitionSpec as P

HEAD = 128
INNER = 4
LANES = 256
KEY_ROWS = 256
STAT_ROWS = 144
NEGATIVE = -1e30
DEAD_VALUE = 1e30
DEAD_BOUND = 1e29
VMEM_BYTES = 16 * 1024 * 1024
F32 = jnp.float32
BF16 = jnp.bfloat16


def dot(left, right):
    return jnp.dot(left, right, preferred_element_type=F32)


def turned(block):
    return block.astype(F32).T.astype(BF16)


def values_with_ones(values):
    rows = values.shape[0]
    return jnp.concatenate([turned(values), jnp.ones((STAT_ROWS - HEAD, rows), BF16)], axis=0)


def own_kernel(exp_scale, len_ref, q_ref, grad_ref, kv_ref, qt_ref, qr_ref, gt_ref, p_ref, m_ref, ot_ref):
    tokens = q_ref.shape[0]
    heads = q_ref.shape[1] // HEAD
    length = len_ref[0, 0]
    live = lax.broadcasted_iota(jnp.int32, (tokens, HEAD), 0) < length
    values = values_with_ones(kv_ref[:, HEAD:])
    key_row = lax.broadcasted_iota(jnp.int32, (tokens, tokens), 0)
    query_row = lax.broadcasted_iota(jnp.int32, (tokens, tokens), 1)
    allowed = (key_row <= query_row) & (key_row < length)
    for head in range(heads):
        span = slice(head * HEAD, (head + 1) * HEAD)
        place = slice(head * tokens, (head + 1) * tokens)
        queries = q_ref[:, span]
        queries_t = turned(queries)
        qr_ref[place, :] = queries
        qt_ref[:, place] = queries_t
        gt_ref[:, place] = jnp.where(live, grad_ref[:, span].astype(F32), 0.0).T.astype(BF16)
        scores = jnp.where(allowed, dot(kv_ref[:, :HEAD], queries_t) * exp_scale, NEGATIVE)
        top = jnp.max(scores, axis=0, keepdims=True)
        weights = jnp.exp(scores - top).astype(BF16)
        p_ref[:, place] = weights
        m_ref[:, place] = top
        ot_ref[:, place] = dot(values, weights)


def forward_kernel(exp_scale, slots, lim_ref, kv_ref, qt_ref, m0_ref, ot0_ref, p_ref, m_ref, ot_ref, s_now):
    rows = kv_ref.shape[0]
    width = qt_ref.shape[1]
    row_values = kv_ref[:, HEAD:]
    values = values_with_ones(row_values)
    block = (lax.broadcasted_iota(jnp.int32, (rows, HEAD), 0) // slots) * INNER + lim_ref[0, 1]
    dead = (row_values.astype(F32) > DEAD_BOUND) | (block >= lim_ref[0, 0])
    bias = jnp.where(dead, NEGATIVE, 0.0)
    peak = jnp.full((8, width), NEGATIVE, F32)
    for start in range(0, rows, KEY_ROWS):
        span = slice(start, start + KEY_ROWS)
        wide = jnp.concatenate([bias[span]] * (width // HEAD), axis=1)
        scores = dot(kv_ref[span, :HEAD], qt_ref[...]) * exp_scale + wide
        s_now[span, :] = scores
        peak = jnp.maximum(peak, jnp.max(scores.reshape(KEY_ROWS // 8, 8, width), axis=0))
    before = m0_ref[...]
    top = jnp.maximum(before, jnp.max(peak, axis=0, keepdims=True))
    m_ref[...] = top
    total = ot0_ref[...] * jnp.exp(before - top)
    for start in range(0, rows, KEY_ROWS):
        span = slice(start, start + KEY_ROWS)
        weights = jnp.exp(s_now[span, :] - top).astype(BF16)
        p_ref[span, :] = weights
        total = total + dot(values[:, span], weights)
    ot_ref[...] = total


def middle_kernel(len_ref, ot_ref, gt_ref, out_ref, inv_ref, delta_ref):
    tokens = out_ref.shape[0]
    heads = out_ref.shape[1] // HEAD
    live = lax.broadcasted_iota(jnp.int32, (tokens, HEAD), 0) < len_ref[0, 0]
    for head in range(heads):
        span = slice(head * HEAD, (head + 1) * HEAD)
        place = slice(head * tokens, (head + 1) * tokens)
        inverse = 1.0 / ot_ref[HEAD : HEAD + 1, place]
        attended = ot_ref[:HEAD, place] * inverse
        out_ref[:, span] = jnp.where(live, attended.T, 0.0).astype(BF16)
        inv_ref[:, place] = inverse
        delta_ref[:, place] = jnp.sum(gt_ref[:, place].astype(F32) * attended, axis=0, keepdims=True)


def backward_kernel(scale, kv_ref, p_ref, mc_ref, m_ref, inv_ref, delta_ref, gt_ref, qr_ref, dq0_ref, dkv_ref, dq_ref, gt_now, gr_now, ds_now):
    keys_t = turned(kv_ref[:, :HEAD])
    values = kv_ref[:, HEAD:]
    width = qr_ref.shape[0]
    factor = jnp.exp(mc_ref[...] - m_ref[...]) * inv_ref[...]
    shift = delta_ref[...] * factor
    for start in range(0, width, HEAD):
        place = slice(start, start + HEAD)
        scaled = gt_ref[:, place].astype(F32) * factor[:, place]
        gt_now[:, place] = scaled.astype(BF16)
        gr_now[place, :] = scaled.T.astype(BF16)
    for start in range(0, width, LANES):
        place = slice(start, start + LANES)
        grad_soft = dot(values, gt_now[:, place])
        grad_scores = (p_ref[:, place].astype(F32) * (grad_soft - shift[:, place])).astype(BF16)
        ds_now[:, place] = grad_scores
        dq_ref[:, place] = dq0_ref[:, place] + dot(keys_t, grad_scores)
    dkv_ref[:, HEAD:] = dot(p_ref[...], gr_now[...]).astype(dkv_ref.dtype)
    dkv_ref[:, :HEAD] = (dot(ds_now[...], qr_ref[...]) * scale).astype(dkv_ref.dtype)


def whole(array):
    zeros = (0,) * array.ndim
    return pl.BlockSpec(array.shape, lambda *_: zeros)


def scalar_spec():
    return pl.BlockSpec(memory_space=pltpu.SMEM)


def params():
    return pltpu.CompilerParams(vmem_limit_bytes=VMEM_BYTES)


def shape_of(shape, dtype):
    return jax.ShapeDtypeStruct(shape, dtype)


def own_call(length, queries, grads, kv):
    tokens, width = queries.shape
    columns = tokens * (width // HEAD)
    outs = [
        shape_of((HEAD, columns), BF16),
        shape_of((columns, HEAD), BF16),
        shape_of((HEAD, columns), BF16),
        shape_of((tokens, columns), BF16),
        shape_of((1, columns), F32),
        shape_of((STAT_ROWS, columns), F32),
    ]
    return pl.pallas_call(
        functools.partial(own_kernel, 1.0 / math.sqrt(HEAD)),
        grid=(1,),
        out_shape=outs,
        in_specs=[scalar_spec(), whole(queries), whole(grads), whole(kv)],
        out_specs=[whole(item) for item in outs],
        compiler_params=params(),
        cost_estimate=pl.CostEstimate(
            flops=4 * tokens * columns * HEAD, bytes_accessed=3_000_000, transcendentals=tokens * columns
        ),
    )(length, queries, grads, kv)


def forward_call(place, kv, slots, queries_t, top, out_t):
    rows = kv.shape[0]
    columns = queries_t.shape[1]
    outs = [shape_of((rows, columns), BF16), shape_of(top.shape, F32), shape_of(out_t.shape, F32)]
    return pl.pallas_call(
        functools.partial(forward_kernel, 1.0 / math.sqrt(HEAD), slots),
        grid=(1,),
        out_shape=outs,
        in_specs=[scalar_spec(), whole(kv), whole(queries_t), whole(top), whole(out_t)],
        out_specs=[whole(item) for item in outs],
        scratch_shapes=[pltpu.VMEM((rows, columns), F32)],
        compiler_params=params(),
        cost_estimate=pl.CostEstimate(
            flops=20 * rows * columns * HEAD,
            bytes_accessed=2 * rows * (columns + 256),
            transcendentals=rows * columns,
        ),
    )(place, kv, queries_t, top, out_t)


def middle_call(length, out_t, grads_t, tokens):
    columns = out_t.shape[1]
    outs = [
        shape_of((tokens, columns // tokens * HEAD), BF16),
        shape_of((1, columns), F32),
        shape_of((1, columns), F32),
    ]
    return pl.pallas_call(
        middle_kernel,
        grid=(1,),
        out_shape=outs,
        in_specs=[scalar_spec(), whole(out_t), whole(grads_t)],
        out_specs=[whole(item) for item in outs],
        compiler_params=params(),
        cost_estimate=pl.CostEstimate(flops=columns * HEAD * 4, bytes_accessed=2_000_000, transcendentals=0),
    )(length, out_t, grads_t)


def backward_call(kv, weights, tops, top, inverse, delta, grads_t, queries, dq_t, dtype):
    rows, width = kv.shape
    columns = queries.shape[0]
    operands = (kv, weights, tops, top, inverse, delta, grads_t, queries, dq_t)
    outs = [shape_of((rows, width), dtype), shape_of(dq_t.shape, F32)]
    return pl.pallas_call(
        functools.partial(backward_kernel, 1.0 / math.sqrt(HEAD)),
        grid=(1,),
        out_shape=outs,
        in_specs=[whole(item) for item in operands],
        out_specs=[whole(item) for item in outs],
        scratch_shapes=[
            pltpu.VMEM((HEAD, columns), BF16),
            pltpu.VMEM((columns, HEAD), BF16),
            pltpu.VMEM((rows, columns), BF16),
        ],
        compiler_params=params(),
        cost_estimate=pl.CostEstimate(
            flops=32 * rows * columns * HEAD,
            bytes_accessed=2 * rows * (columns + 512),
            transcendentals=0,
        ),
    )(*operands)


def per_device(frames, proj_w, text_q, text_k, text_v, frame_count, text_len, grad_out):
    frame_rows = frames.shape[1]
    text_rows = text_q.shape[1]
    proj_rows = proj_w.shape[0]
    ctx_size = lax.axis_size("ctx")
    sections = lax.axis_size("section")
    outer = ctx_size // INNER
    my_index = lax.axis_index("ctx")
    my_inner = my_index % INNER
    my_section = lax.axis_index("section")
    outer_groups = [[o * INNER + i for o in range(outer)] for i in range(INNER)]
    shifts = (2, 1, INNER - 1)
    sources = [my_inner] + [(my_inner + INNER - shift) % INNER for shift in shifts]

    def along_outer(array):
        return lax.all_to_all(
            array, "ctx", split_axis=0, concat_axis=0, tiled=True, axis_index_groups=outer_groups
        )

    def along_inner(array, shift):
        pairs = [
            (o * INNER + i, o * INNER + (i + shift) % INNER) for o in range(outer) for i in range(INNER)
        ]
        return lax.ppermute(array, "ctx", pairs)

    wide_groups = [
        [side * ctx_size + o * INNER + i for side in range(sections) for o in range(outer)] for i in range(INNER)
    ]

    def along_wide(array):
        return lax.all_to_all(
            array, ("section", "ctx"), split_axis=0, concat_axis=0, tiled=True, axis_index_groups=wide_groups
        )

    def copies(block):
        return jnp.broadcast_to(block[None], (outer,) + block.shape)

    def inner_spread(block):
        return [block] + [along_inner(block, shift) for shift in shifts]

    def inner_sum(parts):
        moved = [parts[0]] + [along_inner(part, INNER - shift) for part, shift in zip(parts[1:], shifts)]
        return sum(part.astype(F32) for part in moved)

    def outer_sum(total):
        return along_outer(total.astype(BF16)).astype(F32).sum(axis=0)

    def marked(values, count):
        slot = lax.broadcasted_iota(jnp.int32, values.shape, 0)
        return jnp.where(slot < count, values, jnp.asarray(DEAD_VALUE, BF16))

    def tied(values, *others):
        return lax.optimization_barrier((values,) + others)[0]

    features = frames[0]
    slices = features.reshape(frame_rows, sections, outer, INNER, proj_rows)
    slices = slices.transpose(3, 0, 1, 2, 4).reshape(INNER, frame_rows, outer * sections * proj_rows)

    def feature_slice(inner):
        return lax.dynamic_index_in_dim(slices, inner, 0, False)

    features_now = jnp.concatenate([feature_slice(inner) for inner in sources], axis=1)

    text_kv = jnp.concatenate([text_k[0], marked(text_v[0], text_len[0, 0])], axis=1)
    width = text_kv.shape[1]
    wide = sections * outer
    first = along_wide(jnp.broadcast_to(proj_w[None], (wide,) + proj_w.shape))
    proj_column = first.reshape(wide * proj_rows, width)
    text_column = along_outer(copies(tied(text_kv, first))).reshape(outer * text_rows, width)
    near = [proj_column]
    inner_features = [feature_slice(my_inner)]
    for shift in shifts:
        sent = feature_slice((my_inner + shift) % INNER).reshape(-1, width)
        moved = along_inner(jnp.concatenate([proj_column, sent], axis=0), shift)
        near.append(moved[: wide * proj_rows])
        inner_features.append(moved[wide * proj_rows :].reshape(frame_rows, -1))
    weights_now = jnp.concatenate(near, axis=0)
    text_parts = [text_column] + list(lax.optimization_barrier(inner_spread(tied(text_column, weights_now))[1:]))

    queries_t, queries, grads_t, p_own, m_own, out_t = own_call(text_len, text_q[0], grad_out[0], text_kv)

    def forward(part, source, limit, slots, top, out_t):
        place = jnp.stack([limit, source]).astype(jnp.int32).reshape(1, 2)
        weights_t, top, out_t = forward_call(place, part, slots, queries_t, top, out_t)
        return (part, weights_t, top), top, out_t

    visual = dot(tied(features_now, text_column), weights_now).astype(BF16)
    visual = jnp.concatenate([visual[:, :HEAD], marked(visual[:, HEAD:], frame_count[0, 0])], axis=1)
    top = tied(m_own, visual)
    kept, top, out_t = forward(text_parts[0], sources[0], my_index, text_rows, top, out_t)
    kept_text = [kept]
    visual_column = along_outer(copies(visual)).reshape(outer * frame_rows, width)
    visual_parts = inner_spread(visual_column)

    tp_size = lax.axis_size("tp")
    tp_index = lax.axis_index("tp")
    order = jnp.stack(sources)
    back = jnp.zeros((INNER,), jnp.int32).at[order].set(jnp.arange(INNER, dtype=jnp.int32))
    weights = weights_now.reshape(INNER, sections, outer, proj_rows, width)
    weights = jnp.take(weights, back, axis=0).transpose(1, 2, 0, 3, 4).reshape(tp_size, -1, width).transpose(0, 2, 1)
    top, weights = lax.optimization_barrier((top, weights))
    for part, source in zip(text_parts[1:], sources[1:]):
        kept, top, out_t = forward(part, source, my_index, text_rows, top, out_t)
        kept_text.append(kept)
    kept_visual = []
    for part, source in zip(visual_parts, sources):
        kept, top, out_t = forward(part, source, my_index + 1, frame_rows, top, out_t)
        kept_visual.append(kept)
    attn_out, inverse, delta = middle_call(text_len, out_t, grads_t, text_rows)
    dq_t = jnp.zeros((HEAD, queries.shape[0]), F32)
    common = (top, inverse, delta, grads_t, queries)

    def backward(kept, dq_t):
        return backward_call(*kept, *common, dq_t, BF16)

    dkv_visual = [None] * INNER
    for index in (1, 2, 3, 0):
        dkv_visual[index], dq_t = backward(kept_visual[index], dq_t)
    dkv_text = [None] * INNER
    for index in (1, 2, 3):
        dkv_text[index], dq_t = backward(kept_text[index], dq_t)
    visual_sum = inner_sum(dkv_visual).reshape(outer, frame_rows, width).astype(BF16)
    moved_text = [along_inner(part, INNER - shift) for part, shift in zip(dkv_text[1:], shifts)]
    dq_t = tied(dq_t, visual_sum, moved_text[0])
    dkv_text[0], dq_t = backward(kept_text[0], dq_t)
    dq_t = tied(dq_t, moved_text[1])
    dkv_own, dq_t = backward_call(text_kv, p_own, m_own, *common, dq_t, F32)
    visual_grad = tied(outer_sum(visual_sum).astype(BF16), dq_t)

    visual_near = inner_spread(visual_grad)
    text_sum = sum(part.astype(F32) for part in [dkv_text[0]] + moved_text)
    text_sum = text_sum.reshape(outer, text_rows, width).astype(BF16)
    text_grad = (outer_sum(text_sum) + dkv_own).astype(BF16)

    def frame_part(owner):
        return dot(visual_grad, lax.dynamic_index_in_dim(weights, owner, 0, False))

    d_frames = frame_part(tp_index).astype(BF16).astype(F32)
    for flip in range(1, tp_size):
        pairs = [(i, i ^ flip) for i in range(tp_size)]
        d_frames = d_frames + lax.ppermute(frame_part(tp_index ^ flip).astype(BF16), "tp", pairs).astype(F32)
    d_frames = d_frames.astype(BF16)[None]
    proj_terms = dot(jnp.concatenate(inner_features, axis=0).T, jnp.concatenate(visual_near, axis=0))
    proj_terms = tied(proj_terms.astype(BF16).reshape(wide, proj_rows, width), text_grad, d_frames)
    d_proj_w = along_wide(proj_terms).astype(F32).sum(axis=0)
    d_text_q = (dq_t * (1.0 / math.sqrt(HEAD))).reshape(HEAD, -1, text_rows).transpose(2, 1, 0)
    d_text_q = d_text_q.astype(BF16).reshape(1, text_rows, -1)

    return (attn_out[None], d_text_q, text_grad[None, :, :HEAD], text_grad[None, :, HEAD:], d_frames, d_proj_w)


def solution(mesh):
    in_specs = (
        P("section", "ctx", None),
        P(("section", "ctx"), "tp"),
        P("section", "ctx", "tp"),
        P("section", "ctx", "tp"),
        P("section", "ctx", "tp"),
        P("section", "ctx"),
        P("section", "ctx"),
        P("section", "ctx", "tp"),
    )
    out_specs = (
        P("section", "ctx", "tp"),
        P("section", "ctx", "tp"),
        P("section", "ctx", "tp"),
        P("section", "ctx", "tp"),
        P("section", "ctx", "tp"),
        P(("section", "ctx"), "tp"),
    )
    return jax.shard_map(
        per_device, mesh=mesh, in_specs=in_specs, out_specs=out_specs, check_vma=False
    )
```

```python
import functools
import math

import jax
import jax.numpy as jnp
from jax import lax
from jax.experimental import pallas as pl
from jax.experimental.pallas import tpu as pltpu
from jax.sharding import PartitionSpec as P

HEAD = 128
INNER = 4
LANES = 256
KEY_ROWS = 256
STAT_ROWS = 144
NEGATIVE = -1e30
DEAD_VALUE = 1e30
DEAD_BOUND = 1e29
VMEM_BYTES = 24 * 1024 * 1024
F32 = jnp.float32
BF16 = jnp.bfloat16


def dot(left, right):
    return jnp.dot(left, right, preferred_element_type=F32)


def turned(block):
    return block.astype(F32).T.astype(BF16)


def values_with_ones(values):
    rows = values.shape[0]
    return jnp.concatenate([turned(values), jnp.ones((STAT_ROWS - HEAD, rows), BF16)], axis=0)


def own_kernel(exp_scale, len_ref, q_ref, grad_ref, kv_ref, qt_ref, qr_ref, gt_ref, p_ref, m_ref, ot_ref):
    tokens = q_ref.shape[0]
    heads = q_ref.shape[1] // HEAD
    length = len_ref[0, 0]
    live = lax.broadcasted_iota(jnp.int32, (tokens, HEAD), 0) < length
    values = values_with_ones(kv_ref[:, HEAD:])
    key_row = lax.broadcasted_iota(jnp.int32, (tokens, tokens), 0)
    query_row = lax.broadcasted_iota(jnp.int32, (tokens, tokens), 1)
    allowed = (key_row <= query_row) & (key_row < length)
    for head in range(heads):
        span = slice(head * HEAD, (head + 1) * HEAD)
        place = slice(head * tokens, (head + 1) * tokens)
        queries = q_ref[:, span]
        queries_t = turned(queries)
        qr_ref[place, :] = queries
        qt_ref[:, place] = queries_t
        gt_ref[:, place] = jnp.where(live, grad_ref[:, span].astype(F32), 0.0).T.astype(BF16)
        scores = jnp.where(allowed, dot(kv_ref[:, :HEAD], queries_t) * exp_scale, NEGATIVE)
        top = jnp.max(scores, axis=0, keepdims=True)
        weights = jnp.exp(scores - top).astype(BF16)
        p_ref[:, place] = weights
        m_ref[:, place] = top
        ot_ref[:, place] = dot(values, weights)


def picked(step, refs, now_ref):
    if len(refs) == 1:
        return refs[0]
    for index, ref in enumerate(refs):

        @pl.when(step == index)
        def _():
            now_ref[...] = ref[...]

    return now_ref


def forward_kernel(exp_scale, slots, parts, lim_ref, *refs):
    qt_ref, m0_ref, ot0_ref, p_ref, mc_ref, m_ref, ot_ref, s_now, kv_now = refs[parts:]
    step = pl.program_id(0)
    kv_ref = picked(step, refs[:parts], kv_now)

    @pl.when(step == 0)
    def _():
        m_ref[...] = m0_ref[...]
        ot_ref[...] = ot0_ref[...]

    rows = kv_ref.shape[0]
    width = qt_ref.shape[1]
    row_values = kv_ref[:, HEAD:]
    values = values_with_ones(row_values)
    block = (lax.broadcasted_iota(jnp.int32, (rows, HEAD), 0) // slots) * INNER + lim_ref[0, 1 + step]
    dead = (row_values.astype(F32) > DEAD_BOUND) | (block >= lim_ref[0, 0])
    bias = jnp.where(dead, NEGATIVE, 0.0)
    peak = jnp.full((8, width), NEGATIVE, F32)
    for start in range(0, rows, KEY_ROWS):
        span = slice(start, start + KEY_ROWS)
        wide = jnp.concatenate([bias[span]] * (width // HEAD), axis=1)
        scores = dot(kv_ref[span, :HEAD], qt_ref[...]) * exp_scale + wide
        s_now[span, :] = scores
        peak = jnp.maximum(peak, jnp.max(scores.reshape(KEY_ROWS // 8, 8, width), axis=0))
    before = m_ref[...]
    top = jnp.maximum(before, jnp.max(peak, axis=0, keepdims=True))
    m_ref[...] = top
    mc_ref[0] = top
    total = ot_ref[...] * jnp.exp(before - top)
    for start in range(0, rows, KEY_ROWS):
        span = slice(start, start + KEY_ROWS)
        weights = jnp.exp(s_now[span, :] - top).astype(BF16)
        p_ref[0, span, :] = weights
        total = total + dot(values[:, span], weights)
    ot_ref[...] = total


def middle_kernel(len_ref, ot_ref, gt_ref, out_ref, inv_ref, delta_ref):
    tokens = out_ref.shape[0]
    heads = out_ref.shape[1] // HEAD
    live = lax.broadcasted_iota(jnp.int32, (tokens, HEAD), 0) < len_ref[0, 0]
    for head in range(heads):
        span = slice(head * HEAD, (head + 1) * HEAD)
        place = slice(head * tokens, (head + 1) * tokens)
        inverse = 1.0 / ot_ref[HEAD : HEAD + 1, place]
        attended = ot_ref[:HEAD, place] * inverse
        out_ref[:, span] = jnp.where(live, attended.T, 0.0).astype(BF16)
        inv_ref[:, place] = inverse
        delta_ref[:, place] = jnp.sum(gt_ref[:, place].astype(F32) * attended, axis=0, keepdims=True)


def backward_kernel(scale, parts, *refs):
    p_ref, mc_ref, m_ref, inv_ref, delta_ref, gt_ref, qr_ref, dq0_ref = refs[parts : parts + 8]
    dkv_refs = refs[parts + 8 : 2 * parts + 8]
    dq_ref, gt_now, gr_now, ds_now, kv_now, dkv_now = refs[2 * parts + 8 :]
    step = pl.program_id(0)
    kv_ref = picked(step, refs[:parts], kv_now)

    @pl.when(step == 0)
    def _():
        dq_ref[...] = dq0_ref[...]

    keys_t = turned(kv_ref[:, :HEAD])
    values = kv_ref[:, HEAD:]
    width = qr_ref.shape[0]
    factor = jnp.exp(mc_ref[0] - m_ref[...]) * inv_ref[...]
    shift = delta_ref[...] * factor
    for start in range(0, width, HEAD):
        place = slice(start, start + HEAD)
        scaled = gt_ref[:, place].astype(F32) * factor[:, place]
        gt_now[:, place] = scaled.astype(BF16)
        gr_now[place, :] = scaled.T.astype(BF16)
    for start in range(0, width, LANES):
        place = slice(start, start + LANES)
        grad_soft = dot(values, gt_now[:, place])
        grad_scores = (p_ref[0, :, place].astype(F32) * (grad_soft - shift[:, place])).astype(BF16)
        ds_now[:, place] = grad_scores
        dq_ref[:, place] = dq_ref[:, place] + dot(keys_t, grad_scores)
    target = dkv_refs[0] if parts == 1 else dkv_now
    target[:, HEAD:] = dot(p_ref[0], gr_now[...]).astype(target.dtype)
    target[:, :HEAD] = (dot(ds_now[...], qr_ref[...]) * scale).astype(target.dtype)
    if parts > 1:
        for index, ref in enumerate(dkv_refs):

            @pl.when(step == index)
            def _():
                ref[...] = dkv_now[...]


def whole(array):
    zeros = (0,) * array.ndim
    return pl.BlockSpec(array.shape, lambda *_: zeros)


def by_part(shape, first=0):
    return pl.BlockSpec((1,) + shape[1:], lambda step: (step + first, 0, 0))


def scalar_spec():
    return pl.BlockSpec(memory_space=pltpu.SMEM)


def params():
    return pltpu.CompilerParams(vmem_limit_bytes=VMEM_BYTES)


def shape_of(shape, dtype):
    return jax.ShapeDtypeStruct(shape, dtype)


def own_call(length, queries, grads, kv):
    tokens, width = queries.shape
    columns = tokens * (width // HEAD)
    outs = [
        shape_of((HEAD, columns), BF16),
        shape_of((columns, HEAD), BF16),
        shape_of((HEAD, columns), BF16),
        shape_of((tokens, columns), BF16),
        shape_of((1, columns), F32),
        shape_of((STAT_ROWS, columns), F32),
    ]
    return pl.pallas_call(
        functools.partial(own_kernel, 1.0 / math.sqrt(HEAD)),
        grid=(1,),
        out_shape=outs,
        in_specs=[scalar_spec(), whole(queries), whole(grads), whole(kv)],
        out_specs=[whole(item) for item in outs],
        compiler_params=params(),
        cost_estimate=pl.CostEstimate(
            flops=4 * tokens * columns * HEAD, bytes_accessed=3_000_000, transcendentals=tokens * columns
        ),
    )(length, queries, grads, kv)


def forward_call(place, parts, slots, queries_t, top, out_t):
    count = len(parts)
    rows, width = parts[0].shape
    columns = queries_t.shape[1]
    outs = [
        shape_of((count, rows, columns), BF16),
        shape_of((count, 1, columns), F32),
        shape_of(top.shape, F32),
        shape_of(out_t.shape, F32),
    ]
    return pl.pallas_call(
        functools.partial(forward_kernel, 1.0 / math.sqrt(HEAD), slots, count),
        grid=(count,),
        out_shape=outs,
        in_specs=[scalar_spec()] + [whole(item) for item in (*parts, queries_t, top, out_t)],
        out_specs=[by_part(outs[0].shape), by_part(outs[1].shape), whole(outs[2]), whole(outs[3])],
        scratch_shapes=[pltpu.VMEM((rows, columns), F32), pltpu.VMEM((rows, width), BF16)],
        compiler_params=params(),
        cost_estimate=pl.CostEstimate(
            flops=20 * count * rows * columns * HEAD,
            bytes_accessed=2 * count * rows * (columns + 256),
            transcendentals=count * rows * columns,
        ),
    )(place, *parts, queries_t, top, out_t)


def middle_call(length, out_t, grads_t, tokens):
    columns = out_t.shape[1]
    outs = [
        shape_of((tokens, columns // tokens * HEAD), BF16),
        shape_of((1, columns), F32),
        shape_of((1, columns), F32),
    ]
    return pl.pallas_call(
        middle_kernel,
        grid=(1,),
        out_shape=outs,
        in_specs=[scalar_spec(), whole(out_t), whole(grads_t)],
        out_specs=[whole(item) for item in outs],
        compiler_params=params(),
        cost_estimate=pl.CostEstimate(flops=columns * HEAD * 4, bytes_accessed=2_000_000, transcendentals=0),
    )(length, out_t, grads_t)


def backward_call(parts, first, weights, tops, top, inverse, delta, grads_t, queries, dq_t, dtype=BF16):
    count = len(parts)
    rows, width = parts[0].shape
    columns = queries.shape[0]
    fixed = (top, inverse, delta, grads_t, queries, dq_t)
    outs = [shape_of((rows, width), dtype)] * count + [shape_of(dq_t.shape, F32)]
    return pl.pallas_call(
        functools.partial(backward_kernel, 1.0 / math.sqrt(HEAD), count),
        grid=(count,),
        out_shape=outs,
        in_specs=[whole(item) for item in parts]
        + [by_part(weights.shape, first), by_part(tops.shape, first)]
        + [whole(item) for item in fixed],
        out_specs=[whole(item) for item in outs],
        scratch_shapes=[
            pltpu.VMEM((HEAD, columns), BF16),
            pltpu.VMEM((columns, HEAD), BF16),
            pltpu.VMEM((rows, columns), BF16),
            pltpu.VMEM((rows, width), BF16),
            pltpu.VMEM((rows, width), dtype),
        ],
        compiler_params=params(),
        cost_estimate=pl.CostEstimate(
            flops=32 * count * rows * columns * HEAD,
            bytes_accessed=2 * count * rows * (columns + 512),
            transcendentals=0,
        ),
    )(*parts, weights, tops, *fixed)


def per_device(frames, proj_w, text_q, text_k, text_v, frame_count, text_len, grad_out):
    frame_rows = frames.shape[1]
    text_rows = text_q.shape[1]
    proj_rows = proj_w.shape[0]
    ctx_size = lax.axis_size("ctx")
    sections = lax.axis_size("section")
    outer = ctx_size // INNER
    my_index = lax.axis_index("ctx")
    my_inner = my_index % INNER
    my_section = lax.axis_index("section")
    outer_groups = [[o * INNER + i for o in range(outer)] for i in range(INNER)]
    shifts = (2, 1, INNER - 1)
    sources = [my_inner] + [(my_inner + INNER - shift) % INNER for shift in shifts]

    def along_outer(array):
        return lax.all_to_all(
            array, "ctx", split_axis=0, concat_axis=0, tiled=True, axis_index_groups=outer_groups
        )

    def along_inner(array, shift):
        pairs = [
            (o * INNER + i, o * INNER + (i + shift) % INNER) for o in range(outer) for i in range(INNER)
        ]
        return lax.ppermute(array, "ctx", pairs)

    wide_groups = [
        [side * ctx_size + o * INNER + i for side in range(sections) for o in range(outer)] for i in range(INNER)
    ]

    def along_wide(array):
        return lax.all_to_all(
            array, ("section", "ctx"), split_axis=0, concat_axis=0, tiled=True, axis_index_groups=wide_groups
        )

    def copies(block):
        return jnp.broadcast_to(block[None], (outer,) + block.shape)

    def inner_spread(block):
        return [block] + [along_inner(block, shift) for shift in shifts]

    def inner_sum(parts):
        moved = [parts[0]] + [along_inner(part, INNER - shift) for part, shift in zip(parts[1:], shifts)]
        return sum(part.astype(F32) for part in moved)

    def outer_sum(total):
        return along_outer(total.astype(BF16)).astype(F32).sum(axis=0)

    def marked(values, count):
        slot = lax.broadcasted_iota(jnp.int32, values.shape, 0)
        return jnp.where(slot < count, values, jnp.asarray(DEAD_VALUE, BF16))

    def tied(values, *others):
        return lax.optimization_barrier((values,) + others)[0]

    features = frames[0]
    slices = features.reshape(frame_rows, sections, outer, INNER, proj_rows)
    slices = slices.transpose(3, 0, 1, 2, 4).reshape(INNER, frame_rows, outer * sections * proj_rows)

    def feature_slice(inner):
        return lax.dynamic_index_in_dim(slices, inner, 0, False)

    features_now = jnp.concatenate([feature_slice(inner) for inner in sources], axis=1)

    text_kv = jnp.concatenate([text_k[0], marked(text_v[0], text_len[0, 0])], axis=1)
    width = text_kv.shape[1]
    wide = sections * outer
    first = along_wide(jnp.broadcast_to(proj_w[None], (wide,) + proj_w.shape))
    proj_column = first.reshape(wide * proj_rows, width)
    text_column = along_outer(copies(tied(text_kv, first))).reshape(outer * text_rows, width)
    near = [proj_column]
    inner_features = [feature_slice(my_inner)]
    for shift in shifts:
        sent = feature_slice((my_inner + shift) % INNER).reshape(-1, width)
        moved = along_inner(jnp.concatenate([proj_column, sent], axis=0), shift)
        near.append(moved[: wide * proj_rows])
        inner_features.append(moved[wide * proj_rows :].reshape(frame_rows, -1))
    weights_now = jnp.concatenate(near, axis=0)
    text_parts = [text_column] + list(lax.optimization_barrier(inner_spread(tied(text_column, weights_now))[1:]))

    queries_t, queries, grads_t, p_own, m_own, out_t = own_call(text_len, text_q[0], grad_out[0], text_kv)

    def forward(parts, owners, limit, slots, top, out_t):
        place = jnp.stack([limit] + owners).astype(jnp.int32).reshape(1, -1)
        return forward_call(place, parts, slots, queries_t, top, out_t)

    visual = dot(tied(features_now, text_column), weights_now).astype(BF16)
    visual = jnp.concatenate([visual[:, :HEAD], marked(visual[:, HEAD:], frame_count[0, 0])], axis=1)
    top = tied(m_own, visual)
    p_near, m_near, top, out_t = forward(text_parts[:1], sources[:1], my_index, text_rows, top, out_t)
    visual_column = along_outer(copies(visual)).reshape(outer * frame_rows, width)
    visual_parts = inner_spread(visual_column)

    tp_size = lax.axis_size("tp")
    tp_index = lax.axis_index("tp")
    order = jnp.stack(sources)
    back = jnp.zeros((INNER,), jnp.int32).at[order].set(jnp.arange(INNER, dtype=jnp.int32))
    weights = weights_now.reshape(INNER, sections, outer, proj_rows, width)
    weights = jnp.take(weights, back, axis=0).transpose(1, 2, 0, 3, 4).reshape(tp_size, -1, width).transpose(0, 2, 1)
    top, weights = lax.optimization_barrier((top, weights))
    p_text, m_text, top, out_t = forward(text_parts[1:], sources[1:], my_index, text_rows, top, out_t)
    p_visual, m_visual, top, out_t = forward(visual_parts, sources, my_index + 1, frame_rows, top, out_t)
    attn_out, inverse, delta = middle_call(text_len, out_t, grads_t, text_rows)
    dq_t = jnp.zeros((HEAD, queries.shape[0]), F32)
    common = (top, inverse, delta, grads_t, queries)

    *dkv_visual, dq_t = backward_call(visual_parts[1:], 1, p_visual, m_visual, *common, dq_t)
    dkv_visual_own, dq_t = backward_call(visual_parts[:1], 0, p_visual, m_visual, *common, dq_t)
    *dkv_text, dq_t = backward_call(text_parts[1:], 0, p_text, m_text, *common, dq_t)
    dkv_visual = [dkv_visual_own] + dkv_visual
    visual_sum = inner_sum(dkv_visual).reshape(outer, frame_rows, width).astype(BF16)
    moved_text = [along_inner(part, INNER - shift) for part, shift in zip(dkv_text, shifts)]
    dq_t = tied(dq_t, visual_sum)
    dkv_near, dq_t = backward_call(text_parts[:1], 0, p_near, m_near, *common, dq_t)
    dkv_own, dq_t = backward_call([text_kv], 0, p_own[None], m_own[None], *common, dq_t, F32)
    visual_grad = tied(outer_sum(visual_sum).astype(BF16), dq_t)

    visual_near = inner_spread(visual_grad)
    text_sum = sum(part.astype(F32) for part in [dkv_near] + moved_text)
    text_sum = text_sum.reshape(outer, text_rows, width).astype(BF16)
    text_grad = (outer_sum(text_sum) + dkv_own).astype(BF16)

    def frame_part(owner):
        return dot(visual_grad, lax.dynamic_index_in_dim(weights, owner, 0, False))

    d_frames = frame_part(tp_index).astype(BF16).astype(F32)
    for flip in range(1, tp_size):
        pairs = [(i, i ^ flip) for i in range(tp_size)]
        d_frames = d_frames + lax.ppermute(frame_part(tp_index ^ flip).astype(BF16), "tp", pairs).astype(F32)
    d_frames = d_frames.astype(BF16)[None]
    proj_terms = dot(jnp.concatenate(inner_features, axis=0).T, jnp.concatenate(visual_near, axis=0))
    proj_terms = tied(proj_terms.astype(BF16).reshape(wide, proj_rows, width), text_grad, d_frames)
    d_proj_w = along_wide(proj_terms).astype(F32).sum(axis=0)
    d_text_q = (dq_t * (1.0 / math.sqrt(HEAD))).reshape(HEAD, -1, text_rows).transpose(2, 1, 0)
    d_text_q = d_text_q.astype(BF16).reshape(1, text_rows, -1)

    return (attn_out[None], d_text_q, text_grad[None, :, :HEAD], text_grad[None, :, HEAD:], d_frames, d_proj_w)


def solution(mesh):
    in_specs = (
        P("section", "ctx", None),
        P(("section", "ctx"), "tp"),
        P("section", "ctx", "tp"),
        P("section", "ctx", "tp"),
        P("section", "ctx", "tp"),
        P("section", "ctx"),
        P("section", "ctx"),
        P("section", "ctx", "tp"),
    )
    out_specs = (
        P("section", "ctx", "tp"),
        P("section", "ctx", "tp"),
        P("section", "ctx", "tp"),
        P("section", "ctx", "tp"),
        P("section", "ctx", "tp"),
        P(("section", "ctx"), "tp"),
    )
    return jax.shard_map(
        per_device, mesh=mesh, in_specs=in_specs, out_specs=out_specs, check_vma=False
    )
```

```python
import functools
import math

import jax
import jax.numpy as jnp
from jax import lax
from jax.experimental import pallas as pl
from jax.experimental.pallas import tpu as pltpu
from jax.sharding import PartitionSpec as P

HEAD = 128
INNER = 4
LANES = 256
KEY_ROWS = 256
STAT_ROWS = 144
NEGATIVE = -1e30
DEAD_VALUE = 1e30
DEAD_BOUND = 1e29
VMEM_BYTES = 24 * 1024 * 1024
F32 = jnp.float32
BF16 = jnp.bfloat16


def dot(left, right):
    return jnp.dot(left, right, preferred_element_type=F32)


def turned(block):
    return block.astype(F32).T.astype(BF16)


def values_with_ones(values):
    rows = values.shape[0]
    return jnp.concatenate([turned(values), jnp.ones((STAT_ROWS - HEAD, rows), BF16)], axis=0)


def own_kernel(exp_scale, len_ref, q_ref, grad_ref, kv_ref, qt_ref, qr_ref, gt_ref, p_ref, m_ref, ot_ref):
    tokens = q_ref.shape[0]
    heads = q_ref.shape[1] // HEAD
    length = len_ref[0, 0]
    live = lax.broadcasted_iota(jnp.int32, (tokens, HEAD), 0) < length
    values = values_with_ones(kv_ref[:, HEAD:])
    key_row = lax.broadcasted_iota(jnp.int32, (tokens, tokens), 0)
    query_row = lax.broadcasted_iota(jnp.int32, (tokens, tokens), 1)
    allowed = (key_row <= query_row) & (key_row < length)
    for head in range(heads):
        span = slice(head * HEAD, (head + 1) * HEAD)
        place = slice(head * tokens, (head + 1) * tokens)
        queries = q_ref[:, span]
        queries_t = turned(queries)
        qr_ref[place, :] = queries
        qt_ref[:, place] = queries_t
        gt_ref[:, place] = jnp.where(live, grad_ref[:, span].astype(F32), 0.0).T.astype(BF16)
        scores = jnp.where(allowed, dot(kv_ref[:, :HEAD], queries_t) * exp_scale, NEGATIVE)
        top = jnp.max(scores, axis=0, keepdims=True)
        weights = jnp.exp(scores - top).astype(BF16)
        p_ref[:, place] = weights
        m_ref[:, place] = top
        ot_ref[:, place] = dot(values, weights)


def picked(step, refs, now_ref):
    if len(refs) == 1:
        return refs[0]
    for index, ref in enumerate(refs):

        @pl.when(step == index)
        def _():
            now_ref[...] = ref[...]

    return now_ref


def forward_kernel(exp_scale, slots, parts, lim_ref, *refs):
    qt_ref, m0_ref, ot0_ref, p_ref, mc_ref, m_ref, ot_ref, s_now, kv_now = refs[parts:]
    step = pl.program_id(0)
    kv_ref = picked(step, refs[:parts], kv_now)

    @pl.when(step == 0)
    def _():
        m_ref[...] = m0_ref[...]
        ot_ref[...] = ot0_ref[...]

    rows = kv_ref.shape[0]
    width = qt_ref.shape[1]
    row_values = kv_ref[:, HEAD:]
    values = values_with_ones(row_values)
    block = (lax.broadcasted_iota(jnp.int32, (rows, HEAD), 0) // slots) * INNER + lim_ref[0, 1 + step]
    dead = (row_values.astype(F32) > DEAD_BOUND) | (block >= lim_ref[0, 0])
    bias = jnp.where(dead, NEGATIVE, 0.0)
    peak = jnp.full((8, width), NEGATIVE, F32)
    for start in range(0, rows, KEY_ROWS):
        span = slice(start, start + KEY_ROWS)
        wide = jnp.concatenate([bias[span]] * (width // HEAD), axis=1)
        scores = dot(kv_ref[span, :HEAD], qt_ref[...]) * exp_scale + wide
        s_now[span, :] = scores
        peak = jnp.maximum(peak, jnp.max(scores.reshape(KEY_ROWS // 8, 8, width), axis=0))
    before = m_ref[...]
    top = jnp.maximum(before, jnp.max(peak, axis=0, keepdims=True))
    m_ref[...] = top
    mc_ref[0] = top
    total = ot_ref[...] * jnp.exp(before - top)
    for start in range(0, rows, KEY_ROWS):
        span = slice(start, start + KEY_ROWS)
        weights = jnp.exp(s_now[span, :] - top).astype(BF16)
        p_ref[0, span, :] = weights
        total = total + dot(values[:, span], weights)
    ot_ref[...] = total


def middle_kernel(len_ref, ot_ref, gt_ref, out_ref, inv_ref, delta_ref):
    tokens = out_ref.shape[0]
    heads = out_ref.shape[1] // HEAD
    live = lax.broadcasted_iota(jnp.int32, (tokens, HEAD), 0) < len_ref[0, 0]
    for head in range(heads):
        span = slice(head * HEAD, (head + 1) * HEAD)
        place = slice(head * tokens, (head + 1) * tokens)
        inverse = 1.0 / ot_ref[HEAD : HEAD + 1, place]
        attended = ot_ref[:HEAD, place] * inverse
        out_ref[:, span] = jnp.where(live, attended.T, 0.0).astype(BF16)
        inv_ref[:, place] = inverse
        delta_ref[:, place] = jnp.sum(gt_ref[:, place].astype(F32) * attended, axis=0, keepdims=True)


def backward_kernel(scale, parts, *refs):
    p_ref, mc_ref, m_ref, inv_ref, delta_ref, gt_ref, qr_ref, dq0_ref = refs[parts : parts + 8]
    dkv_refs = refs[parts + 8 : 2 * parts + 8]
    dq_ref, gt_now, ds_now, kv_now, dkv_now = refs[2 * parts + 8 :]
    step = pl.program_id(0)
    kv_ref = picked(step, refs[:parts], kv_now)

    @pl.when(step == 0)
    def _():
        dq_ref[...] = dq0_ref[...]

    keys_t = turned(kv_ref[:, :HEAD])
    values = kv_ref[:, HEAD:]
    width = qr_ref.shape[0]
    factor = jnp.exp(mc_ref[0] - m_ref[...]) * inv_ref[...]
    shift = delta_ref[...] * factor
    for start in range(0, width, HEAD):
        place = slice(start, start + HEAD)
        scaled = gt_ref[:, place].astype(F32) * factor[:, place]
        gt_now[:, place] = scaled.astype(BF16)
    for start in range(0, width, LANES):
        place = slice(start, start + LANES)
        grad_soft = dot(values, gt_now[:, place])
        grad_scores = (p_ref[0, :, place].astype(F32) * (grad_soft - shift[:, place])).astype(BF16)
        ds_now[:, place] = grad_scores
        dq_ref[:, place] = dq_ref[:, place] + dot(keys_t, grad_scores)
    target = dkv_refs[0] if parts == 1 else dkv_now
    target[:, HEAD:] = lax.dot_general(
        p_ref[0], gt_now[...], (((1,), (1,)), ((), ())), preferred_element_type=F32
    ).astype(target.dtype)
    target[:, :HEAD] = (dot(ds_now[...], qr_ref[...]) * scale).astype(target.dtype)
    if parts > 1:
        for index, ref in enumerate(dkv_refs):

            @pl.when(step == index)
            def _():
                ref[...] = dkv_now[...]


def whole(array):
    zeros = (0,) * array.ndim
    return pl.BlockSpec(array.shape, lambda *_: zeros)


def by_part(shape, first=0):
    return pl.BlockSpec((1,) + shape[1:], lambda step: (step + first, 0, 0))


def scalar_spec():
    return pl.BlockSpec(memory_space=pltpu.SMEM)


def params():
    return pltpu.CompilerParams(vmem_limit_bytes=VMEM_BYTES)


def shape_of(shape, dtype):
    return jax.ShapeDtypeStruct(shape, dtype)


def own_call(length, queries, grads, kv):
    tokens, width = queries.shape
    columns = tokens * (width // HEAD)
    outs = [
        shape_of((HEAD, columns), BF16),
        shape_of((columns, HEAD), BF16),
        shape_of((HEAD, columns), BF16),
        shape_of((tokens, columns), BF16),
        shape_of((1, columns), F32),
        shape_of((STAT_ROWS, columns), F32),
    ]
    return pl.pallas_call(
        functools.partial(own_kernel, 1.0 / math.sqrt(HEAD)),
        grid=(1,),
        out_shape=outs,
        in_specs=[scalar_spec(), whole(queries), whole(grads), whole(kv)],
        out_specs=[whole(item) for item in outs],
        compiler_params=params(),
        cost_estimate=pl.CostEstimate(
            flops=4 * tokens * columns * HEAD, bytes_accessed=3_000_000, transcendentals=tokens * columns
        ),
    )(length, queries, grads, kv)


def forward_call(place, parts, slots, queries_t, top, out_t):
    count = len(parts)
    rows, width = parts[0].shape
    columns = queries_t.shape[1]
    outs = [
        shape_of((count, rows, columns), BF16),
        shape_of((count, 1, columns), F32),
        shape_of(top.shape, F32),
        shape_of(out_t.shape, F32),
    ]
    return pl.pallas_call(
        functools.partial(forward_kernel, 1.0 / math.sqrt(HEAD), slots, count),
        grid=(count,),
        out_shape=outs,
        in_specs=[scalar_spec()] + [whole(item) for item in (*parts, queries_t, top, out_t)],
        out_specs=[by_part(outs[0].shape), by_part(outs[1].shape), whole(outs[2]), whole(outs[3])],
        scratch_shapes=[pltpu.VMEM((rows, columns), F32), pltpu.VMEM((rows, width), BF16)],
        compiler_params=params(),
        cost_estimate=pl.CostEstimate(
            flops=20 * count * rows * columns * HEAD,
            bytes_accessed=2 * count * rows * (columns + 256),
            transcendentals=count * rows * columns,
        ),
    )(place, *parts, queries_t, top, out_t)


def middle_call(length, out_t, grads_t, tokens):
    columns = out_t.shape[1]
    outs = [
        shape_of((tokens, columns // tokens * HEAD), BF16),
        shape_of((1, columns), F32),
        shape_of((1, columns), F32),
    ]
    return pl.pallas_call(
        middle_kernel,
        grid=(1,),
        out_shape=outs,
        in_specs=[scalar_spec(), whole(out_t), whole(grads_t)],
        out_specs=[whole(item) for item in outs],
        compiler_params=params(),
        cost_estimate=pl.CostEstimate(flops=columns * HEAD * 4, bytes_accessed=2_000_000, transcendentals=0),
    )(length, out_t, grads_t)


def backward_call(parts, first, weights, tops, top, inverse, delta, grads_t, queries, dq_t, dtype=BF16):
    count = len(parts)
    rows, width = parts[0].shape
    columns = queries.shape[0]
    fixed = (top, inverse, delta, grads_t, queries, dq_t)
    outs = [shape_of((rows, width), dtype)] * count + [shape_of(dq_t.shape, F32)]
    return pl.pallas_call(
        functools.partial(backward_kernel, 1.0 / math.sqrt(HEAD), count),
        grid=(count,),
        out_shape=outs,
        in_specs=[whole(item) for item in parts]
        + [by_part(weights.shape, first), by_part(tops.shape, first)]
        + [whole(item) for item in fixed],
        out_specs=[whole(item) for item in outs],
        scratch_shapes=[
            pltpu.VMEM((HEAD, columns), BF16),
            pltpu.VMEM((rows, columns), BF16),
            pltpu.VMEM((rows, width), BF16),
            pltpu.VMEM((rows, width), dtype),
        ],
        compiler_params=params(),
        cost_estimate=pl.CostEstimate(
            flops=32 * count * rows * columns * HEAD,
            bytes_accessed=2 * count * rows * (columns + 512),
            transcendentals=0,
        ),
    )(*parts, weights, tops, *fixed)


def per_device(frames, proj_w, text_q, text_k, text_v, frame_count, text_len, grad_out):
    frame_rows = frames.shape[1]
    text_rows = text_q.shape[1]
    proj_rows = proj_w.shape[0]
    ctx_size = lax.axis_size("ctx")
    sections = lax.axis_size("section")
    outer = ctx_size // INNER
    my_index = lax.axis_index("ctx")
    my_inner = my_index % INNER
    my_section = lax.axis_index("section")
    outer_groups = [[o * INNER + i for o in range(outer)] for i in range(INNER)]
    shifts = (2, 1, INNER - 1)
    sources = [my_inner] + [(my_inner + INNER - shift) % INNER for shift in shifts]

    def along_outer(array):
        return lax.all_to_all(
            array, "ctx", split_axis=0, concat_axis=0, tiled=True, axis_index_groups=outer_groups
        )

    def along_inner(array, shift):
        pairs = [
            (o * INNER + i, o * INNER + (i + shift) % INNER) for o in range(outer) for i in range(INNER)
        ]
        return lax.ppermute(array, "ctx", pairs)

    wide_groups = [
        [side * ctx_size + o * INNER + i for side in range(sections) for o in range(outer)] for i in range(INNER)
    ]

    def along_wide(array):
        return lax.all_to_all(
            array, ("section", "ctx"), split_axis=0, concat_axis=0, tiled=True, axis_index_groups=wide_groups
        )

    def copies(block):
        return jnp.broadcast_to(block[None], (outer,) + block.shape)

    def inner_spread(block):
        return [block] + [along_inner(block, shift) for shift in shifts]

    def inner_sum(parts):
        moved = [parts[0]] + [along_inner(part, INNER - shift) for part, shift in zip(parts[1:], shifts)]
        return sum(part.astype(F32) for part in moved)

    def outer_sum(total):
        return along_outer(total.astype(BF16)).astype(F32).sum(axis=0)

    def marked(values, count):
        slot = lax.broadcasted_iota(jnp.int32, values.shape, 0)
        return jnp.where(slot < count, values, jnp.asarray(DEAD_VALUE, BF16))

    def tied(values, *others):
        return lax.optimization_barrier((values,) + others)[0]

    features = frames[0]
    slices = features.reshape(frame_rows, sections, outer, INNER, proj_rows)
    slices = slices.transpose(3, 0, 1, 2, 4).reshape(INNER, frame_rows, outer * sections * proj_rows)

    def feature_slice(inner):
        return lax.dynamic_index_in_dim(slices, inner, 0, False)

    features_now = jnp.concatenate([feature_slice(inner) for inner in sources], axis=1)

    text_kv = jnp.concatenate([text_k[0], marked(text_v[0], text_len[0, 0])], axis=1)
    width = text_kv.shape[1]
    wide = sections * outer
    first = along_wide(jnp.broadcast_to(proj_w[None], (wide,) + proj_w.shape))
    proj_column = first.reshape(wide * proj_rows, width)
    text_column = along_outer(copies(tied(text_kv, first))).reshape(outer * text_rows, width)
    near = [proj_column]
    inner_features = [feature_slice(my_inner)]
    for shift in shifts:
        sent = feature_slice((my_inner + shift) % INNER).reshape(-1, width)
        moved = along_inner(jnp.concatenate([proj_column, sent], axis=0), shift)
        near.append(moved[: wide * proj_rows])
        inner_features.append(moved)
    weights_now = jnp.concatenate(near, axis=0)
    text_parts = [text_column] + list(lax.optimization_barrier(inner_spread(tied(text_column, weights_now))[1:]))

    queries_t, queries, grads_t, p_own, m_own, out_t = own_call(text_len, text_q[0], grad_out[0], text_kv)

    def forward(parts, owners, limit, slots, top, out_t):
        place = jnp.stack([limit] + owners).astype(jnp.int32).reshape(1, -1)
        return forward_call(place, parts, slots, queries_t, top, out_t)

    visual = dot(tied(features_now, text_column), weights_now).astype(BF16)
    weights_kept = tied(weights_now, visual)
    visual = jnp.concatenate([visual[:, :HEAD], marked(visual[:, HEAD:], frame_count[0, 0])], axis=1)
    visual_column = along_outer(copies(visual)).reshape(outer * frame_rows, width)
    visual_parts = inner_spread(visual_column)

    tp_size = lax.axis_size("tp")
    tp_index = lax.axis_index("tp")
    order = jnp.stack(sources)
    back = jnp.zeros((INNER,), jnp.int32).at[order].set(jnp.arange(INNER, dtype=jnp.int32))
    weights = weights_kept.reshape(INNER, sections, outer, proj_rows, width)
    weights = jnp.take(weights, back, axis=0).transpose(1, 2, 0, 3, 4).reshape(tp_size, -1, width).transpose(0, 2, 1)
    top, weights = lax.optimization_barrier((m_own, weights))
    p_text, m_text, top, out_t = forward(text_parts, sources, my_index, text_rows, top, out_t)
    p_visual, m_visual, top, out_t = forward(visual_parts, sources, my_index + 1, frame_rows, top, out_t)
    attn_out, inverse, delta = middle_call(text_len, out_t, grads_t, text_rows)
    dq_t = jnp.zeros((HEAD, queries.shape[0]), F32)
    common = (top, inverse, delta, grads_t, queries)

    *dkv_visual, dq_t = backward_call(visual_parts[1:], 1, p_visual, m_visual, *common, dq_t)
    dkv_visual_own, dq_t = backward_call(visual_parts[:1], 0, p_visual, m_visual, *common, dq_t)
    *dkv_text, dq_t = backward_call(text_parts[1:], 1, p_text, m_text, *common, dq_t)
    dkv_visual = [dkv_visual_own] + dkv_visual
    visual_sum = inner_sum(dkv_visual).reshape(outer, frame_rows, width).astype(BF16)
    moved_text = [along_inner(part, INNER - shift) for part, shift in zip(dkv_text, shifts)]
    dq_t = tied(dq_t, visual_sum)
    dkv_near, dq_t = backward_call(text_parts[:1], 0, p_text, m_text, *common, dq_t)
    dkv_own, dq_t = backward_call([text_kv], 0, p_own[None], m_own[None], *common, dq_t, F32)
    visual_grad = tied(outer_sum(visual_sum).astype(BF16), dq_t)
    late = lax.optimization_barrier((inner_features[1:], dq_t))[0]
    inner_features[1:] = [item[wide * proj_rows :].reshape(frame_rows, -1) for item in late]

    visual_near = inner_spread(visual_grad)
    early = sum(part.astype(F32) for part in [dkv_near] + moved_text[:-1])
    early, last_moved = lax.optimization_barrier((early, moved_text[-1]))
    text_sum = early + last_moved.astype(F32)
    text_sum = text_sum.reshape(outer, text_rows, width).astype(BF16)
    text_grad = (outer_sum(text_sum) + dkv_own).astype(BF16)

    def frame_part(owner):
        return dot(visual_grad, lax.dynamic_index_in_dim(weights, owner, 0, False))

    d_frames = frame_part(tp_index).astype(BF16).astype(F32)
    for flip in range(1, tp_size):
        pairs = [(i, i ^ flip) for i in range(tp_size)]
        d_frames = d_frames + lax.ppermute(frame_part(tp_index ^ flip).astype(BF16), "tp", pairs).astype(F32)
    d_frames = d_frames.astype(BF16)[None]
    proj_terms = dot(jnp.concatenate(inner_features, axis=0).T, jnp.concatenate(visual_near, axis=0))
    proj_terms = tied(proj_terms.astype(BF16).reshape(wide, proj_rows, width), text_grad, d_frames)
    d_proj_w = along_wide(proj_terms).astype(F32).sum(axis=0)
    d_text_q = (dq_t * (1.0 / math.sqrt(HEAD))).reshape(HEAD, -1, text_rows).transpose(2, 1, 0)
    d_text_q = d_text_q.astype(BF16).reshape(1, text_rows, -1)

    return (attn_out[None], d_text_q, text_grad[None, :, :HEAD], text_grad[None, :, HEAD:], d_frames, d_proj_w)


def solution(mesh):
    in_specs = (
        P("section", "ctx", None),
        P(("section", "ctx"), "tp"),
        P("section", "ctx", "tp"),
        P("section", "ctx", "tp"),
        P("section", "ctx", "tp"),
        P("section", "ctx"),
        P("section", "ctx"),
        P("section", "ctx", "tp"),
    )
    out_specs = (
        P("section", "ctx", "tp"),
        P("section", "ctx", "tp"),
        P("section", "ctx", "tp"),
        P("section", "ctx", "tp"),
        P("section", "ctx", "tp"),
        P(("section", "ctx"), "tp"),
    )
    return jax.shard_map(
        per_device, mesh=mesh, in_specs=in_specs, out_specs=out_specs, check_vma=False
    )
```

```python
import functools
import math

import jax
import jax.numpy as jnp
from jax import lax
from jax.experimental import pallas as pl
from jax.experimental.pallas import tpu as pltpu
from jax.sharding import PartitionSpec as P

HEAD = 128
INNER = 4
LANES = 256
KEY_ROWS = 256
STAT_ROWS = 144
NEGATIVE = -1e30
DEAD_VALUE = 1e30
DEAD_BOUND = 1e29
VMEM_BYTES = 24 * 1024 * 1024
F32 = jnp.float32
BF16 = jnp.bfloat16


def dot(left, right):
    return jnp.dot(left, right, preferred_element_type=F32)


def turned(block):
    return block.astype(F32).T.astype(BF16)


def values_with_ones(values):
    rows = values.shape[0]
    return jnp.concatenate([turned(values), jnp.ones((STAT_ROWS - HEAD, rows), BF16)], axis=0)


def own_kernel(exp_scale, len_ref, q_ref, grad_ref, kv_ref, qt_ref, qr_ref, gt_ref, p_ref, m_ref, ot_ref):
    tokens = q_ref.shape[0]
    heads = q_ref.shape[1] // HEAD
    length = len_ref[0, 0]
    live = lax.broadcasted_iota(jnp.int32, (tokens, HEAD), 0) < length
    values = values_with_ones(kv_ref[:, HEAD:])
    key_row = lax.broadcasted_iota(jnp.int32, (tokens, tokens), 0)
    query_row = lax.broadcasted_iota(jnp.int32, (tokens, tokens), 1)
    allowed = (key_row <= query_row) & (key_row < length)
    for head in range(heads):
        span = slice(head * HEAD, (head + 1) * HEAD)
        place = slice(head * tokens, (head + 1) * tokens)
        queries = q_ref[:, span]
        queries_t = turned(queries)
        qr_ref[place, :] = queries
        qt_ref[:, place] = queries_t
        gt_ref[:, place] = jnp.where(live, grad_ref[:, span].astype(F32), 0.0).T.astype(BF16)
        scores = jnp.where(allowed, dot(kv_ref[:, :HEAD], queries_t) * exp_scale, NEGATIVE)
        top = jnp.max(scores, axis=0, keepdims=True)
        weights = jnp.exp(scores - top).astype(BF16)
        p_ref[:, place] = weights
        m_ref[:, place] = top
        ot_ref[:, place] = dot(values, weights)


def picked(step, refs, now_ref):
    if len(refs) == 1:
        return refs[0]
    for index, ref in enumerate(refs):

        @pl.when(step == index)
        def _():
            now_ref[...] = ref[...]

    return now_ref


def forward_kernel(exp_scale, slots, parts, lim_ref, *refs):
    qt_ref, m0_ref, ot0_ref, p_ref, mc_ref, m_ref, ot_ref, s_now, kv_now = refs[parts:]
    step = pl.program_id(0)
    kv_ref = picked(step, refs[:parts], kv_now)

    @pl.when(step == 0)
    def _():
        m_ref[...] = m0_ref[...]
        ot_ref[...] = ot0_ref[...]

    rows = kv_ref.shape[0]
    width = qt_ref.shape[1]
    row_values = kv_ref[:, HEAD:]
    values = values_with_ones(row_values)
    block = (lax.broadcasted_iota(jnp.int32, (rows, HEAD), 0) // slots) * INNER + lim_ref[0, 1 + step]
    dead = (row_values.astype(F32) > DEAD_BOUND) | (block >= lim_ref[0, 0])
    bias = jnp.where(dead, NEGATIVE, 0.0)
    peak = jnp.full((8, width), NEGATIVE, F32)
    for start in range(0, rows, KEY_ROWS):
        span = slice(start, start + KEY_ROWS)
        wide = jnp.concatenate([bias[span]] * (width // HEAD), axis=1)
        scores = dot(kv_ref[span, :HEAD], qt_ref[...]) * exp_scale + wide
        s_now[span, :] = scores
        peak = jnp.maximum(peak, jnp.max(scores.reshape(KEY_ROWS // 8, 8, width), axis=0))
    before = m_ref[...]
    top = jnp.maximum(before, jnp.max(peak, axis=0, keepdims=True))
    m_ref[...] = top
    mc_ref[0] = top
    total = ot_ref[...] * jnp.exp(before - top)
    for start in range(0, rows, KEY_ROWS):
        span = slice(start, start + KEY_ROWS)
        weights = jnp.exp(s_now[span, :] - top).astype(BF16)
        p_ref[0, span, :] = weights
        total = total + dot(values[:, span], weights)
    ot_ref[...] = total


def middle_kernel(len_ref, ot_ref, gt_ref, out_ref, inv_ref, delta_ref):
    tokens = out_ref.shape[0]
    heads = out_ref.shape[1] // HEAD
    live = lax.broadcasted_iota(jnp.int32, (tokens, HEAD), 0) < len_ref[0, 0]
    for head in range(heads):
        span = slice(head * HEAD, (head + 1) * HEAD)
        place = slice(head * tokens, (head + 1) * tokens)
        inverse = 1.0 / ot_ref[HEAD : HEAD + 1, place]
        attended = ot_ref[:HEAD, place] * inverse
        out_ref[:, span] = jnp.where(live, attended.T, 0.0).astype(BF16)
        inv_ref[:, place] = inverse
        delta_ref[:, place] = jnp.sum(gt_ref[:, place].astype(F32) * attended, axis=0, keepdims=True)


def backward_kernel(scale, parts, *refs):
    p_ref, mc_ref, m_ref, inv_ref, delta_ref, gt_ref, qr_ref, dq0_ref = refs[parts : parts + 8]
    dkv_refs = refs[parts + 8 : 2 * parts + 8]
    dq_ref, gt_now, ds_now, kv_now, dkv_now = refs[2 * parts + 8 :]
    step = pl.program_id(0)
    kv_ref = picked(step, refs[:parts], kv_now)

    @pl.when(step == 0)
    def _():
        dq_ref[...] = dq0_ref[...]

    keys_t = turned(kv_ref[:, :HEAD])
    values = kv_ref[:, HEAD:]
    width = qr_ref.shape[0]
    factor = jnp.exp(mc_ref[0] - m_ref[...]) * inv_ref[...]
    shift = delta_ref[...] * factor
    for start in range(0, width, HEAD):
        place = slice(start, start + HEAD)
        scaled = gt_ref[:, place].astype(F32) * factor[:, place]
        gt_now[:, place] = scaled.astype(BF16)
    for start in range(0, width, LANES):
        place = slice(start, start + LANES)
        grad_soft = dot(values, gt_now[:, place])
        grad_scores = (p_ref[0, :, place].astype(F32) * (grad_soft - shift[:, place])).astype(BF16)
        ds_now[:, place] = grad_scores
        dq_ref[:, place] = dq_ref[:, place] + dot(keys_t, grad_scores)
    target = dkv_refs[0] if parts == 1 else dkv_now
    target[:, HEAD:] = lax.dot_general(
        p_ref[0], gt_now[...], (((1,), (1,)), ((), ())), preferred_element_type=F32
    ).astype(target.dtype)
    target[:, :HEAD] = (dot(ds_now[...], qr_ref[...]) * scale).astype(target.dtype)
    if parts > 1:
        for index, ref in enumerate(dkv_refs):

            @pl.when(step == index)
            def _():
                ref[...] = dkv_now[...]


def whole(array):
    zeros = (0,) * array.ndim
    return pl.BlockSpec(array.shape, lambda *_: zeros)


def by_part(shape, first=0):
    return pl.BlockSpec((1,) + shape[1:], lambda step: (step + first, 0, 0))


def scalar_spec():
    return pl.BlockSpec(memory_space=pltpu.SMEM)


def params():
    return pltpu.CompilerParams(vmem_limit_bytes=VMEM_BYTES)


def shape_of(shape, dtype):
    return jax.ShapeDtypeStruct(shape, dtype)


def own_call(length, queries, grads, kv):
    tokens, width = queries.shape
    columns = tokens * (width // HEAD)
    outs = [
        shape_of((HEAD, columns), BF16),
        shape_of((columns, HEAD), BF16),
        shape_of((HEAD, columns), BF16),
        shape_of((tokens, columns), BF16),
        shape_of((1, columns), F32),
        shape_of((STAT_ROWS, columns), F32),
    ]
    return pl.pallas_call(
        functools.partial(own_kernel, 1.0 / math.sqrt(HEAD)),
        grid=(1,),
        out_shape=outs,
        in_specs=[scalar_spec(), whole(queries), whole(grads), whole(kv)],
        out_specs=[whole(item) for item in outs],
        compiler_params=params(),
        cost_estimate=pl.CostEstimate(
            flops=4 * tokens * columns * HEAD, bytes_accessed=3_000_000, transcendentals=tokens * columns
        ),
    )(length, queries, grads, kv)


def forward_call(place, parts, slots, queries_t, top, out_t):
    count = len(parts)
    rows, width = parts[0].shape
    columns = queries_t.shape[1]
    outs = [
        shape_of((count, rows, columns), BF16),
        shape_of((count, 1, columns), F32),
        shape_of(top.shape, F32),
        shape_of(out_t.shape, F32),
    ]
    return pl.pallas_call(
        functools.partial(forward_kernel, 1.0 / math.sqrt(HEAD), slots, count),
        grid=(count,),
        out_shape=outs,
        in_specs=[scalar_spec()] + [whole(item) for item in (*parts, queries_t, top, out_t)],
        out_specs=[by_part(outs[0].shape), by_part(outs[1].shape), whole(outs[2]), whole(outs[3])],
        scratch_shapes=[pltpu.VMEM((rows, columns), F32), pltpu.VMEM((rows, width), BF16)],
        compiler_params=params(),
        cost_estimate=pl.CostEstimate(
            flops=20 * count * rows * columns * HEAD,
            bytes_accessed=2 * count * rows * (columns + 256),
            transcendentals=count * rows * columns,
        ),
    )(place, *parts, queries_t, top, out_t)


def middle_call(length, out_t, grads_t, tokens):
    columns = out_t.shape[1]
    outs = [
        shape_of((tokens, columns // tokens * HEAD), BF16),
        shape_of((1, columns), F32),
        shape_of((1, columns), F32),
    ]
    return pl.pallas_call(
        middle_kernel,
        grid=(1,),
        out_shape=outs,
        in_specs=[scalar_spec(), whole(out_t), whole(grads_t)],
        out_specs=[whole(item) for item in outs],
        compiler_params=params(),
        cost_estimate=pl.CostEstimate(flops=columns * HEAD * 4, bytes_accessed=2_000_000, transcendentals=0),
    )(length, out_t, grads_t)


def backward_call(parts, first, weights, tops, top, inverse, delta, grads_t, queries, dq_t, dtype=BF16):
    count = len(parts)
    rows, width = parts[0].shape
    columns = queries.shape[0]
    fixed = (top, inverse, delta, grads_t, queries, dq_t)
    outs = [shape_of((rows, width), dtype)] * count + [shape_of(dq_t.shape, F32)]
    return pl.pallas_call(
        functools.partial(backward_kernel, 1.0 / math.sqrt(HEAD), count),
        grid=(count,),
        out_shape=outs,
        in_specs=[whole(item) for item in parts]
        + [by_part(weights.shape, first), by_part(tops.shape, first)]
        + [whole(item) for item in fixed],
        out_specs=[whole(item) for item in outs],
        scratch_shapes=[
            pltpu.VMEM((HEAD, columns), BF16),
            pltpu.VMEM((rows, columns), BF16),
            pltpu.VMEM((rows, width), BF16),
            pltpu.VMEM((rows, width), dtype),
        ],
        compiler_params=params(),
        cost_estimate=pl.CostEstimate(
            flops=32 * count * rows * columns * HEAD,
            bytes_accessed=2 * count * rows * (columns + 512),
            transcendentals=0,
        ),
    )(*parts, weights, tops, *fixed)


def per_device(frames, proj_w, text_q, text_k, text_v, frame_count, text_len, grad_out):
    frame_rows = frames.shape[1]
    text_rows = text_q.shape[1]
    proj_rows = proj_w.shape[0]
    ctx_size = lax.axis_size("ctx")
    sections = lax.axis_size("section")
    outer = ctx_size // INNER
    my_index = lax.axis_index("ctx")
    my_inner = my_index % INNER
    my_section = lax.axis_index("section")
    outer_groups = [[o * INNER + i for o in range(outer)] for i in range(INNER)]
    shifts = (2, 1, INNER - 1)
    sources = [my_inner] + [(my_inner + INNER - shift) % INNER for shift in shifts]

    def along_outer(array):
        return lax.all_to_all(
            array, "ctx", split_axis=0, concat_axis=0, tiled=True, axis_index_groups=outer_groups
        )

    def along_inner(array, shift):
        pairs = [
            (o * INNER + i, o * INNER + (i + shift) % INNER) for o in range(outer) for i in range(INNER)
        ]
        return lax.ppermute(array, "ctx", pairs)

    wide_groups = [
        [side * ctx_size + o * INNER + i for side in range(sections) for o in range(outer)] for i in range(INNER)
    ]

    def along_wide(array):
        return lax.all_to_all(
            array, ("section", "ctx"), split_axis=0, concat_axis=0, tiled=True, axis_index_groups=wide_groups
        )

    def copies(block):
        return jnp.broadcast_to(block[None], (outer,) + block.shape)

    def inner_spread(block):
        return [block] + [along_inner(block, shift) for shift in shifts]

    def inner_sum(parts):
        moved = [parts[0]] + [along_inner(part, INNER - shift) for part, shift in zip(parts[1:], shifts)]
        return sum(part.astype(F32) for part in moved)

    def outer_sum(total):
        return along_outer(total.astype(BF16)).astype(F32).sum(axis=0)

    def marked(values, count):
        slot = lax.broadcasted_iota(jnp.int32, values.shape, 0)
        return jnp.where(slot < count, values, jnp.asarray(DEAD_VALUE, BF16))

    def tied(values, *others):
        return lax.optimization_barrier((values,) + others)[0]

    features = frames[0]
    slices = features.reshape(frame_rows, sections, outer, INNER, proj_rows)
    slices = slices.transpose(3, 0, 1, 2, 4).reshape(INNER, frame_rows, outer * sections * proj_rows)

    def feature_slice(inner):
        return lax.dynamic_index_in_dim(slices, inner, 0, False)

    features_now = jnp.concatenate([feature_slice(inner) for inner in sources], axis=1)

    text_kv = jnp.concatenate([text_k[0], marked(text_v[0], text_len[0, 0])], axis=1)
    width = text_kv.shape[1]
    wide = sections * outer
    first = along_wide(jnp.broadcast_to(proj_w[None], (wide,) + proj_w.shape))
    proj_column = first.reshape(wide * proj_rows, width)
    text_column = along_outer(copies(tied(text_kv, first))).reshape(outer * text_rows, width)
    near = [proj_column]
    inner_features = [feature_slice(my_inner)]
    for shift in shifts:
        sent = feature_slice((my_inner + shift) % INNER).reshape(-1, width)
        moved = along_inner(jnp.concatenate([proj_column, sent], axis=0), shift)
        near.append(moved[: wide * proj_rows])
        inner_features.append(moved)
    weights_now = jnp.concatenate(near, axis=0)
    text_parts = [text_column] + list(lax.optimization_barrier(inner_spread(tied(text_column, weights_now))[1:]))

    queries_t, queries, grads_t, p_own, m_own, out_t = own_call(text_len, text_q[0], grad_out[0], text_kv)

    def forward(parts, owners, limit, slots, top, out_t):
        place = jnp.stack([limit] + owners).astype(jnp.int32).reshape(1, -1)
        return forward_call(place, parts, slots, queries_t, top, out_t)

    visual = dot(tied(features_now, text_column), weights_now).astype(BF16)
    weights_kept = tied(weights_now, visual)
    visual = jnp.concatenate([visual[:, :HEAD], marked(visual[:, HEAD:], frame_count[0, 0])], axis=1)
    visual_column = along_outer(copies(visual)).reshape(outer * frame_rows, width)
    visual_parts = inner_spread(visual_column)

    tp_size = lax.axis_size("tp")
    tp_index = lax.axis_index("tp")
    order = jnp.stack(sources)
    back = jnp.zeros((INNER,), jnp.int32).at[order].set(jnp.arange(INNER, dtype=jnp.int32))
    weights = weights_kept.reshape(INNER, sections, outer, proj_rows, width)
    weights = jnp.take(weights, back, axis=0).transpose(1, 2, 0, 3, 4).reshape(tp_size, -1, width).transpose(0, 2, 1)
    top, weights = lax.optimization_barrier((m_own, weights))
    p_text, m_text, top, out_t = forward(text_parts, sources, my_index, text_rows, top, out_t)
    p_visual, m_visual, top, out_t = forward(visual_parts, sources, my_index + 1, frame_rows, top, out_t)
    attn_out, inverse, delta = middle_call(text_len, out_t, grads_t, text_rows)
    dq_t = jnp.zeros((HEAD, queries.shape[0]), F32)
    common = (top, inverse, delta, grads_t, queries)

    *dkv_visual, dq_t = backward_call(visual_parts[1:], 1, p_visual, m_visual, *common, dq_t)
    *dkv_text, dq_t = backward_call(text_parts[1:], 1, p_text, m_text, *common, dq_t)
    dkv_visual_own, dq_t = backward_call(visual_parts[:1], 0, p_visual, m_visual, *common, dq_t)
    dkv_visual = [dkv_visual_own] + dkv_visual
    visual_sum = inner_sum(dkv_visual).reshape(outer, frame_rows, width).astype(BF16)
    moved_text = [along_inner(part, INNER - shift) for part, shift in zip(dkv_text, shifts)]
    dq_t = tied(dq_t, visual_sum)
    dkv_near, dq_t = backward_call(text_parts[:1], 0, p_text, m_text, *common, dq_t)
    dkv_own, dq_t = backward_call([text_kv], 0, p_own[None], m_own[None], *common, dq_t, F32)
    visual_grad = tied(outer_sum(visual_sum).astype(BF16), dq_t)
    late = lax.optimization_barrier((inner_features[1:], dq_t))[0]
    inner_features[1:] = [item[wide * proj_rows :].reshape(frame_rows, -1) for item in late]

    visual_near = inner_spread(visual_grad)
    early = sum(part.astype(F32) for part in [dkv_near] + moved_text[:-1])
    early, last_moved = lax.optimization_barrier((early, moved_text[-1]))
    text_sum = early + last_moved.astype(F32)
    text_sum = text_sum.reshape(outer, text_rows, width).astype(BF16)
    text_grad = (outer_sum(text_sum) + dkv_own).astype(BF16)

    def frame_part(owner):
        return dot(visual_grad, lax.dynamic_index_in_dim(weights, owner, 0, False))

    d_frames = frame_part(tp_index).astype(BF16).astype(F32)
    for flip in range(1, tp_size):
        pairs = [(i, i ^ flip) for i in range(tp_size)]
        d_frames = d_frames + lax.ppermute(frame_part(tp_index ^ flip).astype(BF16), "tp", pairs).astype(F32)
    d_frames = d_frames.astype(BF16)[None]
    proj_terms = dot(jnp.concatenate(inner_features, axis=0).T, jnp.concatenate(visual_near, axis=0))
    proj_terms = tied(proj_terms.astype(BF16).reshape(wide, proj_rows, width), text_grad, d_frames)
    d_proj_w = along_wide(proj_terms).astype(F32).sum(axis=0)
    d_text_q = (dq_t * (1.0 / math.sqrt(HEAD))).reshape(HEAD, -1, text_rows).transpose(2, 1, 0)
    d_text_q = d_text_q.astype(BF16).reshape(1, text_rows, -1)

    return (attn_out[None], d_text_q, text_grad[None, :, :HEAD], text_grad[None, :, HEAD:], d_frames, d_proj_w)


def solution(mesh):
    in_specs = (
        P("section", "ctx", None),
        P(("section", "ctx"), "tp"),
        P("section", "ctx", "tp"),
        P("section", "ctx", "tp"),
        P("section", "ctx", "tp"),
        P("section", "ctx"),
        P("section", "ctx"),
        P("section", "ctx", "tp"),
    )
    out_specs = (
        P("section", "ctx", "tp"),
        P("section", "ctx", "tp"),
        P("section", "ctx", "tp"),
        P("section", "ctx", "tp"),
        P("section", "ctx", "tp"),
        P(("section", "ctx"), "tp"),
    )
    return jax.shard_map(
        per_device, mesh=mesh, in_specs=in_specs, out_specs=out_specs, check_vma=False
    )
```

```python
import functools
import math

import jax
import jax.numpy as jnp
from jax import lax
from jax.experimental import pallas as pl
from jax.experimental.pallas import tpu as pltpu
from jax.sharding import PartitionSpec as P

HEAD = 128
INNER = 4
LANES = 512
KEY_ROWS = 256
STAT_ROWS = 144
NEGATIVE = -1e30
DEAD_VALUE = 1e30
DEAD_BOUND = 1e29
VMEM_BYTES = 24 * 1024 * 1024
F32 = jnp.float32
BF16 = jnp.bfloat16


def dot(left, right):
    return jnp.dot(left, right, preferred_element_type=F32)


def turned(block):
    return block.astype(F32).T.astype(BF16)


def values_with_ones(values):
    rows = values.shape[0]
    return jnp.concatenate([turned(values), jnp.ones((STAT_ROWS - HEAD, rows), BF16)], axis=0)


def own_kernel(exp_scale, len_ref, q_ref, grad_ref, kv_ref, qt_ref, qr_ref, gt_ref, p_ref, m_ref, ot_ref):
    tokens = q_ref.shape[0]
    heads = q_ref.shape[1] // HEAD
    length = len_ref[0, 0]
    live = lax.broadcasted_iota(jnp.int32, (tokens, HEAD), 0) < length
    values = values_with_ones(kv_ref[:, HEAD:])
    key_row = lax.broadcasted_iota(jnp.int32, (tokens, tokens), 0)
    query_row = lax.broadcasted_iota(jnp.int32, (tokens, tokens), 1)
    allowed = (key_row <= query_row) & (key_row < length)
    for head in range(heads):
        span = slice(head * HEAD, (head + 1) * HEAD)
        place = slice(head * tokens, (head + 1) * tokens)
        queries = q_ref[:, span]
        queries_t = turned(queries)
        qr_ref[place, :] = queries
        qt_ref[:, place] = queries_t
        gt_ref[:, place] = jnp.where(live, grad_ref[:, span].astype(F32), 0.0).T.astype(BF16)
        scores = jnp.where(allowed, dot(kv_ref[:, :HEAD], queries_t) * exp_scale, NEGATIVE)
        top = jnp.max(scores, axis=0, keepdims=True)
        weights = jnp.exp(scores - top).astype(BF16)
        p_ref[:, place] = weights
        m_ref[:, place] = top
        ot_ref[:, place] = dot(values, weights)


def picked(step, refs, now_ref):
    if len(refs) == 1:
        return refs[0]
    for index, ref in enumerate(refs):

        @pl.when(step == index)
        def _():
            now_ref[...] = ref[...]

    return now_ref


def forward_kernel(exp_scale, slots, parts, lim_ref, *refs):
    qt_ref, m0_ref, ot0_ref, p_ref, mc_ref, m_ref, ot_ref, s_now, kv_now = refs[parts:]
    step = pl.program_id(0)
    kv_ref = picked(step, refs[:parts], kv_now)

    @pl.when(step == 0)
    def _():
        m_ref[...] = m0_ref[...]
        ot_ref[...] = ot0_ref[...]

    rows = kv_ref.shape[0]
    width = qt_ref.shape[1]
    row_values = kv_ref[:, HEAD:]
    values = values_with_ones(row_values)
    block = (lax.broadcasted_iota(jnp.int32, (rows, HEAD), 0) // slots) * INNER + lim_ref[0, 1 + step]
    dead = (row_values.astype(F32) > DEAD_BOUND) | (block >= lim_ref[0, 0])
    bias = jnp.where(dead, NEGATIVE, 0.0)
    peak = jnp.full((8, width), NEGATIVE, F32)
    for start in range(0, rows, KEY_ROWS):
        span = slice(start, start + KEY_ROWS)
        wide = jnp.concatenate([bias[span]] * (width // HEAD), axis=1)
        scores = dot(kv_ref[span, :HEAD], qt_ref[...]) * exp_scale + wide
        s_now[span, :] = scores
        peak = jnp.maximum(peak, jnp.max(scores.reshape(KEY_ROWS // 8, 8, width), axis=0))
    before = m_ref[...]
    top = jnp.maximum(before, jnp.max(peak, axis=0, keepdims=True))
    m_ref[...] = top
    mc_ref[0] = top
    total = ot_ref[...] * jnp.exp(before - top)
    for start in range(0, rows, KEY_ROWS):
        span = slice(start, start + KEY_ROWS)
        weights = jnp.exp(s_now[span, :] - top).astype(BF16)
        p_ref[0, span, :] = weights
        total = total + dot(values[:, span], weights)
    ot_ref[...] = total


def middle_kernel(len_ref, ot_ref, gt_ref, out_ref, inv_ref, delta_ref):
    tokens = out_ref.shape[0]
    heads = out_ref.shape[1] // HEAD
    live = lax.broadcasted_iota(jnp.int32, (tokens, HEAD), 0) < len_ref[0, 0]
    for head in range(heads):
        span = slice(head * HEAD, (head + 1) * HEAD)
        place = slice(head * tokens, (head + 1) * tokens)
        inverse = 1.0 / ot_ref[HEAD : HEAD + 1, place]
        attended = ot_ref[:HEAD, place] * inverse
        out_ref[:, span] = jnp.where(live, attended.T, 0.0).astype(BF16)
        inv_ref[:, place] = inverse
        delta_ref[:, place] = jnp.sum(gt_ref[:, place].astype(F32) * attended, axis=0, keepdims=True)


def backward_kernel(scale, parts, *refs):
    p_ref, mc_ref, m_ref, inv_ref, delta_ref, gt_ref, qr_ref, dq0_ref = refs[parts : parts + 8]
    dkv_refs = refs[parts + 8 : 2 * parts + 8]
    dq_ref, gt_now, ds_now, kv_now, dkv_now = refs[2 * parts + 8 :]
    step = pl.program_id(0)
    kv_ref = picked(step, refs[:parts], kv_now)

    @pl.when(step == 0)
    def _():
        dq_ref[...] = dq0_ref[...]

    keys_t = turned(kv_ref[:, :HEAD])
    values = kv_ref[:, HEAD:]
    width = qr_ref.shape[0]
    factor = jnp.exp(mc_ref[0] - m_ref[...]) * inv_ref[...]
    shift = delta_ref[...] * factor
    for start in range(0, width, HEAD):
        place = slice(start, start + HEAD)
        scaled = gt_ref[:, place].astype(F32) * factor[:, place]
        gt_now[:, place] = scaled.astype(BF16)
    for start in range(0, width, LANES):
        place = slice(start, start + LANES)
        grad_soft = dot(values, gt_now[:, place])
        grad_scores = (p_ref[0, :, place].astype(F32) * (grad_soft - shift[:, place])).astype(BF16)
        ds_now[:, place] = grad_scores
        dq_ref[:, place] = dq_ref[:, place] + dot(keys_t, grad_scores)
    target = dkv_refs[0] if parts == 1 else dkv_now
    target[:, HEAD:] = lax.dot_general(
        p_ref[0], gt_now[...], (((1,), (1,)), ((), ())), preferred_element_type=F32
    ).astype(target.dtype)
    target[:, :HEAD] = (dot(ds_now[...], qr_ref[...]) * scale).astype(target.dtype)
    if parts > 1:
        for index, ref in enumerate(dkv_refs):

            @pl.when(step == index)
            def _():
                ref[...] = dkv_now[...]


def whole(array):
    zeros = (0,) * array.ndim
    return pl.BlockSpec(array.shape, lambda *_: zeros)


def by_part(shape, first=0):
    return pl.BlockSpec((1,) + shape[1:], lambda step: (step + first, 0, 0))


def scalar_spec():
    return pl.BlockSpec(memory_space=pltpu.SMEM)


def params():
    return pltpu.CompilerParams(vmem_limit_bytes=VMEM_BYTES)


def shape_of(shape, dtype):
    return jax.ShapeDtypeStruct(shape, dtype)


def own_call(length, queries, grads, kv):
    tokens, width = queries.shape
    columns = tokens * (width // HEAD)
    outs = [
        shape_of((HEAD, columns), BF16),
        shape_of((columns, HEAD), BF16),
        shape_of((HEAD, columns), BF16),
        shape_of((tokens, columns), BF16),
        shape_of((1, columns), F32),
        shape_of((STAT_ROWS, columns), F32),
    ]
    return pl.pallas_call(
        functools.partial(own_kernel, 1.0 / math.sqrt(HEAD)),
        grid=(1,),
        out_shape=outs,
        in_specs=[scalar_spec(), whole(queries), whole(grads), whole(kv)],
        out_specs=[whole(item) for item in outs],
        compiler_params=params(),
        cost_estimate=pl.CostEstimate(
            flops=4 * tokens * columns * HEAD, bytes_accessed=3_000_000, transcendentals=tokens * columns
        ),
    )(length, queries, grads, kv)


def forward_call(place, parts, slots, queries_t, top, out_t):
    count = len(parts)
    rows, width = parts[0].shape
    columns = queries_t.shape[1]
    outs = [
        shape_of((count, rows, columns), BF16),
        shape_of((count, 1, columns), F32),
        shape_of(top.shape, F32),
        shape_of(out_t.shape, F32),
    ]
    return pl.pallas_call(
        functools.partial(forward_kernel, 1.0 / math.sqrt(HEAD), slots, count),
        grid=(count,),
        out_shape=outs,
        in_specs=[scalar_spec()] + [whole(item) for item in (*parts, queries_t, top, out_t)],
        out_specs=[by_part(outs[0].shape), by_part(outs[1].shape), whole(outs[2]), whole(outs[3])],
        scratch_shapes=[pltpu.VMEM((rows, columns), F32), pltpu.VMEM((rows, width), BF16)],
        compiler_params=params(),
        cost_estimate=pl.CostEstimate(
            flops=20 * count * rows * columns * HEAD,
            bytes_accessed=2 * count * rows * (columns + 256),
            transcendentals=count * rows * columns,
        ),
    )(place, *parts, queries_t, top, out_t)


def middle_call(length, out_t, grads_t, tokens):
    columns = out_t.shape[1]
    outs = [
        shape_of((tokens, columns // tokens * HEAD), BF16),
        shape_of((1, columns), F32),
        shape_of((1, columns), F32),
    ]
    return pl.pallas_call(
        middle_kernel,
        grid=(1,),
        out_shape=outs,
        in_specs=[scalar_spec(), whole(out_t), whole(grads_t)],
        out_specs=[whole(item) for item in outs],
        compiler_params=params(),
        cost_estimate=pl.CostEstimate(flops=columns * HEAD * 4, bytes_accessed=2_000_000, transcendentals=0),
    )(length, out_t, grads_t)


def backward_call(parts, first, weights, tops, top, inverse, delta, grads_t, queries, dq_t, dtype=BF16):
    count = len(parts)
    rows, width = parts[0].shape
    columns = queries.shape[0]
    fixed = (top, inverse, delta, grads_t, queries, dq_t)
    outs = [shape_of((rows, width), dtype)] * count + [shape_of(dq_t.shape, F32)]
    return pl.pallas_call(
        functools.partial(backward_kernel, 1.0 / math.sqrt(HEAD), count),
        grid=(count,),
        out_shape=outs,
        in_specs=[whole(item) for item in parts]
        + [by_part(weights.shape, first), by_part(tops.shape, first)]
        + [whole(item) for item in fixed],
        out_specs=[whole(item) for item in outs],
        scratch_shapes=[
            pltpu.VMEM((HEAD, columns), BF16),
            pltpu.VMEM((rows, columns), BF16),
            pltpu.VMEM((rows, width), BF16),
            pltpu.VMEM((rows, width), dtype),
        ],
        compiler_params=params(),
        cost_estimate=pl.CostEstimate(
            flops=32 * count * rows * columns * HEAD,
            bytes_accessed=2 * count * rows * (columns + 512),
            transcendentals=0,
        ),
    )(*parts, weights, tops, *fixed)


def per_device(frames, proj_w, text_q, text_k, text_v, frame_count, text_len, grad_out):
    frame_rows = frames.shape[1]
    text_rows = text_q.shape[1]
    proj_rows = proj_w.shape[0]
    ctx_size = lax.axis_size("ctx")
    sections = lax.axis_size("section")
    outer = ctx_size // INNER
    my_index = lax.axis_index("ctx")
    my_inner = my_index % INNER
    my_section = lax.axis_index("section")
    outer_groups = [[o * INNER + i for o in range(outer)] for i in range(INNER)]
    shifts = (2, 1, INNER - 1)
    sources = [my_inner] + [(my_inner + INNER - shift) % INNER for shift in shifts]

    def along_outer(array):
        return lax.all_to_all(
            array, "ctx", split_axis=0, concat_axis=0, tiled=True, axis_index_groups=outer_groups
        )

    def along_inner(array, shift):
        pairs = [
            (o * INNER + i, o * INNER + (i + shift) % INNER) for o in range(outer) for i in range(INNER)
        ]
        return lax.ppermute(array, "ctx", pairs)

    wide_groups = [
        [side * ctx_size + o * INNER + i for side in range(sections) for o in range(outer)] for i in range(INNER)
    ]

    def along_wide(array):
        return lax.all_to_all(
            array, ("section", "ctx"), split_axis=0, concat_axis=0, tiled=True, axis_index_groups=wide_groups
        )

    def copies(block):
        return jnp.broadcast_to(block[None], (outer,) + block.shape)

    def inner_spread(block):
        return [block] + [along_inner(block, shift) for shift in shifts]

    def inner_sum(parts):
        moved = [parts[0]] + [along_inner(part, INNER - shift) for part, shift in zip(parts[1:], shifts)]
        return sum(part.astype(F32) for part in moved)

    def outer_sum(total):
        return along_outer(total.astype(BF16)).astype(F32).sum(axis=0)

    def marked(values, count):
        slot = lax.broadcasted_iota(jnp.int32, values.shape, 0)
        return jnp.where(slot < count, values, jnp.asarray(DEAD_VALUE, BF16))

    def tied(values, *others):
        return lax.optimization_barrier((values,) + others)[0]

    features = frames[0]
    slices = features.reshape(frame_rows, sections, outer, INNER, proj_rows)
    slices = slices.transpose(3, 0, 1, 2, 4).reshape(INNER, frame_rows, outer * sections * proj_rows)

    def feature_slice(inner):
        return lax.dynamic_index_in_dim(slices, inner, 0, False)

    features_now = jnp.concatenate([feature_slice(inner) for inner in sources], axis=1)

    text_kv = jnp.concatenate([text_k[0], marked(text_v[0], text_len[0, 0])], axis=1)
    width = text_kv.shape[1]
    wide = sections * outer
    first = along_wide(jnp.broadcast_to(proj_w[None], (wide,) + proj_w.shape))
    proj_column = first.reshape(wide * proj_rows, width)
    text_column = along_outer(copies(tied(text_kv, first))).reshape(outer * text_rows, width)
    near = [proj_column]
    inner_features = [feature_slice(my_inner)]
    for shift in shifts:
        sent = feature_slice((my_inner + shift) % INNER).reshape(-1, width)
        moved = along_inner(jnp.concatenate([proj_column, sent], axis=0), shift)
        near.append(moved[: wide * proj_rows])
        inner_features.append(moved)
    weights_now = jnp.concatenate(near, axis=0)
    text_parts = [text_column] + list(lax.optimization_barrier(inner_spread(tied(text_column, weights_now))[1:]))

    queries_t, queries, grads_t, p_own, m_own, out_t = own_call(text_len, text_q[0], grad_out[0], text_kv)

    def forward(parts, owners, limit, slots, top, out_t):
        place = jnp.stack([limit] + owners).astype(jnp.int32).reshape(1, -1)
        return forward_call(place, parts, slots, queries_t, top, out_t)

    visual = dot(tied(features_now, text_column), weights_now).astype(BF16)
    weights_kept = tied(weights_now, visual)
    visual = jnp.concatenate([visual[:, :HEAD], marked(visual[:, HEAD:], frame_count[0, 0])], axis=1)
    visual_column = along_outer(copies(visual)).reshape(outer * frame_rows, width)
    visual_parts = inner_spread(visual_column)

    tp_size = lax.axis_size("tp")
    tp_index = lax.axis_index("tp")
    order = jnp.stack(sources)
    back = jnp.zeros((INNER,), jnp.int32).at[order].set(jnp.arange(INNER, dtype=jnp.int32))
    weights = weights_kept.reshape(INNER, sections, outer, proj_rows, width)
    weights = jnp.take(weights, back, axis=0).transpose(1, 2, 0, 3, 4).reshape(tp_size, -1, width).transpose(0, 2, 1)
    top, weights = lax.optimization_barrier((m_own, weights))
    p_text, m_text, top, out_t = forward(text_parts, sources, my_index, text_rows, top, out_t)
    p_visual, m_visual, top, out_t = forward(visual_parts, sources, my_index + 1, frame_rows, top, out_t)
    attn_out, inverse, delta = middle_call(text_len, out_t, grads_t, text_rows)
    dq_t = jnp.zeros((HEAD, queries.shape[0]), F32)
    common = (top, inverse, delta, grads_t, queries)

    *dkv_visual, dq_t = backward_call(visual_parts[1:], 1, p_visual, m_visual, *common, dq_t)
    *dkv_text, dq_t = backward_call(text_parts[1:], 1, p_text, m_text, *common, dq_t)
    dkv_visual_own, dq_t = backward_call(visual_parts[:1], 0, p_visual, m_visual, *common, dq_t)
    dkv_visual = [dkv_visual_own] + dkv_visual
    visual_sum = inner_sum(dkv_visual).reshape(outer, frame_rows, width).astype(BF16)
    moved_text = [along_inner(part, INNER - shift) for part, shift in zip(dkv_text, shifts)]
    dq_t = tied(dq_t, visual_sum)
    dkv_near, dq_t = backward_call(text_parts[:1], 0, p_text, m_text, *common, dq_t)
    dkv_own, dq_t = backward_call([text_kv], 0, p_own[None], m_own[None], *common, dq_t, F32)
    visual_grad = tied(outer_sum(visual_sum).astype(BF16), dq_t)
    late = lax.optimization_barrier((inner_features[1:], dq_t))[0]
    inner_features[1:] = [item[wide * proj_rows :].reshape(frame_rows, -1) for item in late]

    visual_near = inner_spread(visual_grad)
    early = sum(part.astype(F32) for part in [dkv_near] + moved_text[:-1])
    early, last_moved = lax.optimization_barrier((early, moved_text[-1]))
    text_sum = early + last_moved.astype(F32)
    text_sum = text_sum.reshape(outer, text_rows, width).astype(BF16)
    text_grad = (outer_sum(text_sum) + dkv_own).astype(BF16)

    def frame_part(owner):
        return dot(visual_grad, lax.dynamic_index_in_dim(weights, owner, 0, False))

    d_frames = frame_part(tp_index).astype(BF16).astype(F32)
    for flip in range(1, tp_size):
        pairs = [(i, i ^ flip) for i in range(tp_size)]
        d_frames = d_frames + lax.ppermute(frame_part(tp_index ^ flip).astype(BF16), "tp", pairs).astype(F32)
    d_frames = d_frames.astype(BF16)[None]
    proj_terms = dot(jnp.concatenate(inner_features, axis=0).T, jnp.concatenate(visual_near, axis=0))
    proj_terms = tied(proj_terms.astype(BF16).reshape(wide, proj_rows, width), text_grad, d_frames)
    d_proj_w = along_wide(proj_terms).astype(F32).sum(axis=0)
    d_text_q = (dq_t * (1.0 / math.sqrt(HEAD))).reshape(HEAD, -1, text_rows).transpose(2, 1, 0)
    d_text_q = d_text_q.astype(BF16).reshape(1, text_rows, -1)

    return (attn_out[None], d_text_q, text_grad[None, :, :HEAD], text_grad[None, :, HEAD:], d_frames, d_proj_w)


def solution(mesh):
    in_specs = (
        P("section", "ctx", None),
        P(("section", "ctx"), "tp"),
        P("section", "ctx", "tp"),
        P("section", "ctx", "tp"),
        P("section", "ctx", "tp"),
        P("section", "ctx"),
        P("section", "ctx"),
        P("section", "ctx", "tp"),
    )
    out_specs = (
        P("section", "ctx", "tp"),
        P("section", "ctx", "tp"),
        P("section", "ctx", "tp"),
        P("section", "ctx", "tp"),
        P("section", "ctx", "tp"),
        P(("section", "ctx"), "tp"),
    )
    return jax.shard_map(
        per_device, mesh=mesh, in_specs=in_specs, out_specs=out_specs, check_vma=False
    )
```
